256 devices in a mesh: ctx: 16 (over z, core), grp: 16 (over y, x).
Axes of the slice: x: 4, y: 4, z: 8, core: 2. Of those that a mesh axis runs over, the one named last changes fastest.
Arguments:
- queries: bfloat16 [4096, 36864], P('ctx', 'grp'), may hold values from -20 to 20
- latent_cache: bfloat16 [1024, 36864], P('ctx'), may hold values from -18 to 18
- block_picks: int32 [16, 32], P('ctx'), may hold values from 0 to 1023, as said below
- out_grad: bfloat16 [4096, 32768], P('ctx', 'grp'), may hold values from -16 to 16
Outputs:
- query_grad: bfloat16 [4096, 36864], P('ctx', 'grp')
- latent_grad: bfloat16 [1024, 36864], P(('ctx', 'grp'))
The draws below stay inside these ranges and needn't reach their ends.
Inputs may be any that keep to these rules, and one draw needn't show every extreme that they name: `block_picks`: A row names 32 different blocks. The 1 row of one index of ctx name no block twice, and name at most 4 blocks of any one index's range of 64 blocks, exactly 4 of one such range.
All inputs are finite; a program needn't handle non-finite values.
Results may differ from the reference program's by a relative error of at most 0.023.
Values may be sent and summed in bfloat16 or wider, within the bound.
No kernel may reach another device: no remote copies, remote signals or barrier semaphores. Data moves between devices by JAX's collectives and lax.ppermute only.
A program may use at most 128 MiB of HBM per device.

```python
import math
import jax
import jax.numpy as jnp
from jax import lax

H = 64
DL = 512
DR = 64
BLK = 64
TOPK = 32
QBLK = 256
NB_SHARD = 64
DK = 576
H_DEV = 4
QB_DEV = 1
CAP = 4
QTOT = 4096
NQB = 16
NBLK = 1024
N_CTX = 16
N_GRP = 16


def pick_table(key):
    key = jax.random.fold_in(key, 11)
    pick_total = QB_DEV * TOPK

    def one_group(group_key):
        first_key, second_key, third_key, fourth_key = jax.random.split(group_key, 4)
        hot_shard = jax.random.randint(first_key, (), 0, N_CTX)
        spare_slots = jax.random.permutation(second_key, (N_CTX - 1) * CAP)[:pick_total - CAP]
        spare_shard = spare_slots // CAP
        spare_shard = spare_shard + (spare_shard >= hot_shard).astype(jnp.int32)
        spare_rank = spare_slots % CAP
        shard_ids = jnp.concatenate([jnp.full((CAP,), hot_shard, jnp.int32), spare_shard.astype(jnp.int32)])
        rank_ids = jnp.concatenate([jnp.arange(CAP, dtype=jnp.int32), spare_rank.astype(jnp.int32)])
        block_orders = jax.vmap(lambda shard_key: jax.random.permutation(shard_key, NB_SHARD))(jax.random.split(third_key, N_CTX))
        local_ids = block_orders[shard_ids, rank_ids]
        global_ids = shard_ids * NB_SHARD + local_ids
        shuffle = jax.random.permutation(fourth_key, pick_total)
        return global_ids[shuffle].reshape(QB_DEV, TOPK)
    table = jax.vmap(one_group)(jax.random.split(key, N_CTX))
    return table.reshape(NQB, TOPK).astype(jnp.int32)


def draw_block_picks(key, part):
    return pick_table(key)


def draw_queries(key, part):
    key = jax.random.fold_in(key, 5)
    first_key, second_key = jax.random.split(key)
    scales = jnp.exp(jax.random.uniform(first_key, (QTOT, H, 1), minval=math.log(0.05), maxval=math.log(0.3)))
    values = jnp.clip(jax.random.normal(second_key, (QTOT, H, DK)), -6.0, 6.0) * scales
    return values.reshape(QTOT, H * DK).astype(jnp.bfloat16)


def draw_latent_cache(key, part):
    key = jax.random.fold_in(key, 3)
    first_key, second_key = jax.random.split(key)
    scales = jnp.exp(jax.random.uniform(first_key, (NBLK, BLK, 1), minval=math.log(0.3), maxval=math.log(3.0)))
    values = jnp.clip(jax.random.normal(second_key, (NBLK, BLK, DK)), -6.0, 6.0) * scales
    return values.reshape(NBLK, BLK * DK).astype(jnp.bfloat16)


def block_levels(stream_key, dims, shards, least, high):
    factor_of, own = 1.0, jax.random.fold_in(stream_key, 6)
    for axis_at, shards_of in shards:
        heights = jnp.exp(jax.random.uniform(jax.random.fold_in(own, axis_at), (shards_of,), jnp.float32, least / len(shards), high / len(shards)))
        factor_of = factor_of * jnp.repeat(heights, dims[axis_at] // shards_of).reshape([-1 if axis == axis_at else 1 for axis in range(len(dims))])
    return factor_of


def bell_draw(stream_key, extent, width, most, pieces=(), held_as=jnp.bfloat16):
    drawn = jax.random.normal(stream_key, extent, jnp.float32) * width
    if len(pieces) > 0:
        drawn = block_levels(stream_key, extent, pieces, -0.22, 0.18) * drawn
    return jnp.clip(drawn, min=-most, max=most).astype(held_as)


def setup_inputs(seed: int = 0) -> dict:
    streams_of = jax.random.split(jax.random.key(seed), 5)
    queries = draw_queries(jax.random.fold_in(streams_of[4], 71), 0)
    latent_cache = draw_latent_cache(jax.random.fold_in(streams_of[4], 71), 0)
    block_picks = draw_block_picks(jax.random.fold_in(streams_of[4], 71), 0)
    out_grad = bell_draw(streams_of[3], (QTOT, H * DL), 4.0, 16.0, ((0, 16), (1, 16)))
    return dict(queries=queries, latent_cache=latent_cache, block_picks=block_picks, out_grad=out_grad)


SCORE_SCALE = 192.0 ** -0.5


def reference(queries, latent_cache, block_picks, out_grad):
    cache_blocks = latent_cache.reshape(NBLK, BLK, DK)

    def one_block(total, inputs):
        query_block, grad_block, picks_row = inputs
        block_keys = cache_blocks[picks_row].reshape(TOPK * BLK, DK).astype(jnp.float32)

        def one_group(pair):
            query_part, grad_part = pair
            query_wide = query_part.astype(jnp.float32)
            grad_wide = grad_part.astype(jnp.float32)
            scores = jnp.einsum("qhd,kd->hqk", query_wide, block_keys) * SCORE_SCALE
            attention = jax.nn.softmax(scores, axis=2)
            dprobs = jnp.einsum("qhe,ke->hqk", grad_wide, block_keys[:, :DL])
            inner_sum = jnp.sum(attention * dprobs, axis=2, keepdims=True)
            dscores = (attention * (dprobs - inner_sum) * SCORE_SCALE).astype(jnp.bfloat16)
            probs_low = attention.astype(jnp.bfloat16)
            query_grad = jnp.einsum("hqk,kd->qhd", dscores.astype(jnp.float32), block_keys).astype(jnp.bfloat16)
            key_part = jnp.einsum("hqk,qhd->kd", dscores.astype(jnp.float32), query_wide)
            value_part = jnp.einsum("hqk,qhe->ke", probs_low.astype(jnp.float32), grad_wide)
            partial_value = (key_part + jnp.pad(value_part, ((0, 0), (0, DR)))).astype(jnp.bfloat16)
            return query_grad, partial_value

        query_groups = query_block.reshape(QBLK, N_GRP, H_DEV, DK).transpose(1, 0, 2, 3)
        grad_groups = grad_block.reshape(QBLK, N_GRP, H_DEV, DL).transpose(1, 0, 2, 3)
        query_grads, partials = lax.map(one_group, (query_groups, grad_groups))
        query_grad = query_grads.transpose(1, 0, 2, 3).reshape(QBLK, H * DK)
        summed = jnp.sum(partials.astype(jnp.float32), axis=0).reshape(TOPK, BLK * DK)
        total = total.at[picks_row].add(summed)
        return total, query_grad

    start_total = jnp.zeros((NBLK, BLK * DK), jnp.float32)
    total, query_grads = lax.scan(
        one_block,
        start_total,
        (queries.reshape(NQB, QBLK, H, DK), out_grad.reshape(NQB, QBLK, H, DL), block_picks),
    )
    return query_grads.reshape(QTOT, H * DK), total.astype(jnp.bfloat16)
```

```python
import functools
import jax
import jax.numpy as jnp
from jax import lax
from jax.experimental import pallas as pl
from jax.experimental.pallas import tpu as pltpu
from jax.sharding import PartitionSpec as P

DL = 512
DR = 64
QBLK = 256
DK = 576
SCORE_SCALE = 192.0 ** (-0.5)
LOG2E = 1.4426950408889634
F32 = jnp.float32
BF16 = jnp.bfloat16
NT = (((1,), (1,)), ((), ()))
NN = (((1,), (0,)), ((), ()))
TN = (((0,), (0,)), ((), ()))


def attend_kernel(heads, reps, x_ref, q_ref, g_ref, dq_ref, part_ref,
                  kbuf, ktbuf, qbuf, gbuf, sbuf, dpbuf, dsbuf, pbuf):
    rows = x_ref.shape[0]
    keys = rows * reps
    for r in range(reps):
        piece = x_ref[:, r * DK:(r + 1) * DK]
        kbuf[r * rows:(r + 1) * rows, :] = piece
        ktbuf[:, r * rows:(r + 1) * rows] = piece.T
    for h in range(heads):
        qbuf[h * QBLK:(h + 1) * QBLK, :] = q_ref[:, h * DK:(h + 1) * DK]
        gbuf[h * QBLK:(h + 1) * QBLK, :] = g_ref[:, h * DL:(h + 1) * DL]
    kc = 512
    nc = keys // kc

    def products(h):
        slot = h % 2
        qh = qbuf[h * QBLK:(h + 1) * QBLK, :]
        gh = gbuf[h * QBLK:(h + 1) * QBLK, :]
        for c in range(nc):
            k = kbuf[c * kc:(c + 1) * kc, :]
            sbuf[slot, c * kc:(c + 1) * kc, :] = lax.dot_general(k, qh, NT, preferred_element_type=F32)
            dpbuf[slot, c * kc:(c + 1) * kc, :] = lax.dot_general(k[:, :DL], gh, NT, preferred_element_type=F32)

    def soften(h):
        slot = h % 2
        m = jnp.max(sbuf[slot], axis=0, keepdims=True)
        factor = SCORE_SCALE * LOG2E
        total = jnp.zeros((1, QBLK), F32)
        inner = jnp.zeros((1, QBLK), F32)
        for c in range(nc):
            p = jnp.exp2((sbuf[slot, c * kc:(c + 1) * kc, :] - m) * factor)
            sbuf[slot, c * kc:(c + 1) * kc, :] = p
            total += jnp.sum(p, axis=0, keepdims=True)
            inner += jnp.sum(p * dpbuf[slot, c * kc:(c + 1) * kc, :], axis=0, keepdims=True)
        inv = 1.0 / total
        inner = inner * inv
        for c in range(nc):
            a = sbuf[slot, c * kc:(c + 1) * kc, :] * inv
            d = a * (dpbuf[slot, c * kc:(c + 1) * kc, :] - inner) * SCORE_SCALE
            pbuf[c * kc:(c + 1) * kc, h * QBLK:(h + 1) * QBLK] = a.astype(BF16)
            dsbuf[c * kc:(c + 1) * kc, h * QBLK:(h + 1) * QBLK] = d.astype(BF16)

    products(0)
    for h in range(heads):
        if h + 1 < heads:
            products(h + 1)
        soften(h)
    for r in range(reps):
        ds = dsbuf[r * rows:(r + 1) * rows, :]
        p = pbuf[r * rows:(r + 1) * rows, :]
        kp = lax.dot_general(ds, qbuf[...], NN, preferred_element_type=F32)
        vp = lax.dot_general(p, gbuf[...], NN, preferred_element_type=F32)
        part_ref[:, r * DK:r * DK + DL] = (kp[:, :DL] + vp).astype(BF16)
        part_ref[:, r * DK + DL:(r + 1) * DK] = kp[:, DL:].astype(BF16)
    for h in range(heads):
        dqt = lax.dot_general(ktbuf[...], dsbuf[:, h * QBLK:(h + 1) * QBLK], NN, preferred_element_type=F32)
        dq_ref[:, h * DK:(h + 1) * DK] = dqt.T.astype(BF16)


def attend(x, q, g):
    rows = x.shape[0]
    reps = x.shape[1] // DK
    heads = q.shape[1] // DK
    keys = rows * reps
    vm = pl.BlockSpec(memory_space=pltpu.VMEM)
    return pl.pallas_call(
        functools.partial(attend_kernel, heads, reps),
        out_shape=(jax.ShapeDtypeStruct(q.shape, BF16), jax.ShapeDtypeStruct(x.shape, BF16)),
        in_specs=[vm] * 3,
        out_specs=(vm, vm),
        scratch_shapes=[
            pltpu.VMEM((keys, DK), BF16),
            pltpu.VMEM((DK, keys), BF16),
            pltpu.VMEM((heads * QBLK, DK), BF16),
            pltpu.VMEM((heads * QBLK, DL), BF16),
            pltpu.VMEM((2, keys, QBLK), F32),
            pltpu.VMEM((2, keys, QBLK), F32),
            pltpu.VMEM((keys, heads * QBLK), BF16),
            pltpu.VMEM((keys, heads * QBLK), BF16),
        ],
        compiler_params=pltpu.CompilerParams(vmem_limit_bytes=56 * 1024 * 1024),
        name="attend",
    )(x, q, g)


def serve_kernel(place, picks_ref, cache_ref, out_ref, sums_ref):
    shards, capacity, width = out_ref.shape
    blocks = cache_ref.shape[0]
    slots = shards * capacity
    total = picks_ref.shape[1]
    per = total // shards
    picks = picks_ref[...]
    mine = (picks // blocks) == place[0]
    within = picks % blocks
    first = lax.broadcasted_iota(jnp.int32, (total, total), 0)
    second = lax.broadcasted_iota(jnp.int32, (total, total), 1)
    before = ((first // per == second // per) & (first < second)).astype(BF16)
    marks = jnp.broadcast_to(mine.astype(F32), (8, total)).astype(BF16)
    rank = lax.dot_general(marks, before, NN, preferred_element_type=F32)[:1].astype(jnp.int32)
    slot = lax.broadcasted_iota(jnp.int32, (slots, total), 0)
    asker = lax.broadcasted_iota(jnp.int32, (slots, total), 1) // per
    spot = jnp.where(mine, rank, capacity)
    left = ((slot // capacity == asker) & (slot % capacity == spot)).astype(BF16)
    block = lax.broadcasted_iota(jnp.int32, (blocks, total), 0)
    right = (block == within).astype(BF16)
    chosen = lax.dot_general(left, right, NT, preferred_element_type=F32).astype(BF16)
    sums_ref[...] = lax.dot_general(right, left, NT, preferred_element_type=F32).astype(BF16)
    served = lax.dot_general(chosen, cache_ref[...], NN, preferred_element_type=F32).astype(BF16)
    for c in range(shards):
        out_ref[c] = served[c * capacity:(c + 1) * capacity]


def serve(place, picks, cache, shards, groups):
    blocks, whole = cache.shape
    width = whole // groups
    per = picks.shape[1] // shards
    capacity = 2 * per // shards
    return pl.pallas_call(
        serve_kernel,
        out_shape=(
            jax.ShapeDtypeStruct((shards, capacity, width), BF16),
            jax.ShapeDtypeStruct((blocks, shards * capacity), BF16),
        ),
        grid_spec=pltpu.PrefetchScalarGridSpec(
            num_scalar_prefetch=1,
            grid=(1,),
            in_specs=[
                pl.BlockSpec(picks.shape, lambda i, place: (0, 0)),
                pl.BlockSpec((blocks, width), lambda i, place: (0, place[1])),
            ],
            out_specs=(
                pl.BlockSpec((shards, capacity, width), lambda i, place: (0, 0, 0)),
                pl.BlockSpec((blocks, shards * capacity), lambda i, place: (0, 0)),
            ),
        ),
        name="serve",
    )(place, picks, cache)


def compact_kernel(block_count, copies, picks_ref, recv_ref, out_ref, spot_ref):
    shards, capacity, width = recv_ref.shape
    slots = shards * capacity
    per = picks_ref.shape[1]
    picks = picks_ref[...]
    holder = picks // block_count
    first = lax.broadcasted_iota(jnp.int32, (per, per), 0)
    second = lax.broadcasted_iota(jnp.int32, (per, per), 1)
    shard = lax.broadcasted_iota(jnp.int32, (shards, per), 0)
    held = shard == holder
    before = (first < second).astype(BF16)
    counts = lax.dot_general(held.astype(BF16), before, NN, preferred_element_type=F32)
    rank = jnp.sum(jnp.where(held, counts, 0.0), axis=0, keepdims=True).astype(jnp.int32)
    slot = lax.broadcasted_iota(jnp.int32, (slots, per), 0)
    spots = (slot == holder * capacity + rank).astype(BF16)
    spot_ref[...] = spots
    recv = jnp.concatenate([recv_ref[c] for c in range(shards)], axis=0)
    picked = lax.dot_general(spots, recv, TN, preferred_element_type=F32).astype(BF16)
    for e in range(copies):
        out_ref[e * per:(e + 1) * per, :] = picked


def compact(picks, recv, block_count, copies):
    per = picks.shape[1]
    shards, capacity, width = recv.shape
    vm = pl.BlockSpec(memory_space=pltpu.VMEM)
    return pl.pallas_call(
        functools.partial(compact_kernel, block_count, copies),
        out_shape=(
            jax.ShapeDtypeStruct((copies * per, width), BF16),
            jax.ShapeDtypeStruct((shards * capacity, per), BF16),
        ),
        in_specs=[vm, vm],
        out_specs=(vm, vm),
        compiler_params=pltpu.CompilerParams(vmem_limit_bytes=32 * 1024 * 1024),
        name="compact",
    )(picks, recv)


def fold_kernel(part_ref, spot_ref, out_ref):
    shards, capacity, width = out_ref.shape
    per = spot_ref.shape[1]
    total = part_ref[:per, :].astype(F32)
    for e in range(1, part_ref.shape[0] // per):
        total += part_ref[e * per:(e + 1) * per, :].astype(F32)
    placed = lax.dot_general(
        spot_ref[...], total.astype(BF16), NN, preferred_element_type=F32
    ).astype(BF16)
    for c in range(shards):
        out_ref[c] = placed[c * capacity:(c + 1) * capacity]


def fold(parts, spots, shards):
    width = parts.shape[1]
    vm = pl.BlockSpec(memory_space=pltpu.VMEM)
    return pl.pallas_call(
        fold_kernel,
        out_shape=jax.ShapeDtypeStruct((shards, spots.shape[0] // shards, width), BF16),
        in_specs=[vm, vm],
        out_specs=vm,
        compiler_params=pltpu.CompilerParams(vmem_limit_bytes=32 * 1024 * 1024),
        name="fold",
    )(parts, spots)


def collect_kernel(recv_ref, sums_ref, out_ref):
    recv = jnp.concatenate([recv_ref[c] for c in range(recv_ref.shape[0])], axis=0)
    total = lax.dot_general(sums_ref[...], recv, NN, preferred_element_type=F32).astype(BF16)
    for e in range(out_ref.shape[0]):
        size = out_ref.shape[1]
        out_ref[e] = total[e * size:(e + 1) * size]


def collect(recv, sums, groups):
    width = recv.shape[2]
    vm = pl.BlockSpec(memory_space=pltpu.VMEM)
    return pl.pallas_call(
        collect_kernel,
        out_shape=jax.ShapeDtypeStruct((groups, sums.shape[0] // groups, width), BF16),
        in_specs=[vm, vm],
        out_specs=vm,
        compiler_params=pltpu.CompilerParams(vmem_limit_bytes=32 * 1024 * 1024),
        name="collect",
    )(recv, sums)


def on_device(queries, latent_cache, block_picks, out_grad):
    shards = lax.axis_size("ctx")
    groups = lax.axis_size("grp")
    block_count = latent_cache.shape[0]
    place = jnp.stack([lax.axis_index("ctx"), lax.axis_index("grp")]).astype(jnp.int32)
    every = lax.all_gather(block_picks, "ctx", axis=1, tiled=True)
    served, sums = serve(place, every, latent_cache, shards, groups)
    fetched = lax.all_to_all(served, "ctx", split_axis=0, concat_axis=0, tiled=True)
    picked, spots = compact(block_picks, fetched, block_count, groups)
    keys = lax.all_to_all(picked, "grp", split_axis=0, concat_axis=0, tiled=True)
    query_grad, partial = attend(keys, queries, out_grad)
    parts = lax.all_to_all(partial, "grp", split_axis=0, concat_axis=0, tiled=True)
    placed = fold(parts, spots, shards)
    returned = lax.all_to_all(placed, "ctx", split_axis=0, concat_axis=0, tiled=True)
    owned = collect(returned, sums, groups)
    final = lax.all_to_all(owned, "grp", split_axis=0, concat_axis=0, tiled=True)
    latent_grad = jnp.swapaxes(final, 0, 1).reshape(block_count // groups, latent_cache.shape[1])
    return (query_grad, latent_grad)


def solution(mesh):
    placed = (P("ctx", "grp"), P("ctx", None), P("ctx", None), P("ctx", "grp"))
    return jax.shard_map(
        on_device,
        mesh=mesh,
        in_specs=placed,
        out_specs=(P("ctx", "grp"), P(("ctx", "grp"), None)),
        check_vma=False,
    )
```

```python
import functools
import jax
import jax.numpy as jnp
from jax import lax
from jax.experimental import pallas as pl
from jax.experimental.pallas import tpu as pltpu
from jax.sharding import PartitionSpec as P

DL = 512
DR = 64
QBLK = 256
DK = 576
SCORE_SCALE = 192.0 ** (-0.5)
LOG2E = 1.4426950408889634
F32 = jnp.float32
BF16 = jnp.bfloat16
NT = (((1,), (1,)), ((), ()))
NN = (((1,), (0,)), ((), ()))
TN = (((0,), (0,)), ((), ()))


def scores_kernel(heads, reps, near_ref, far_ref, q_ref, g_ref, ds_ref, p_ref, far_out, qbuf, gbuf,
                  kbuf, sbuf, dpbuf):
    rows = near_ref.shape[0]
    keys = 2 * rows * reps
    for half, ref in enumerate((near_ref, far_ref)):
        for r in range(reps):
            at = (half * reps + r) * rows
            kbuf[at:at + rows, :] = ref[:, r * DK:(r + 1) * DK]
    for h in range(heads):
        qbuf[h * QBLK:(h + 1) * QBLK, :] = q_ref[:, h * DK:(h + 1) * DK]
        gbuf[h * QBLK:(h + 1) * QBLK, :] = g_ref[:, h * DL:(h + 1) * DL]
    kc = 512
    nc = keys // kc
    factor = SCORE_SCALE * LOG2E

    def products(h, c, peak):
        slot = h % 2
        qh = qbuf[h * QBLK:(h + 1) * QBLK, :]
        gh = gbuf[h * QBLK:(h + 1) * QBLK, :]
        k = kbuf[c * kc:(c + 1) * kc, :]
        s = lax.dot_general(k, qh, NT, preferred_element_type=F32)
        sbuf[slot, c * kc:(c + 1) * kc, :] = s
        dpbuf[slot, c * kc:(c + 1) * kc, :] = lax.dot_general(k[:, :DL], gh, NT, preferred_element_type=F32)
        top = jnp.max(s.reshape(kc // 8, 8, QBLK), axis=0)
        return top if peak is None else jnp.maximum(peak, top)

    def weigh(h, c, m, total, inner):
        slot = h % 2
        p = jnp.exp2((sbuf[slot, c * kc:(c + 1) * kc, :] - m) * factor)
        sbuf[slot, c * kc:(c + 1) * kc, :] = p
        d = p * dpbuf[slot, c * kc:(c + 1) * kc, :]
        total += jnp.sum(p.reshape(kc // 8, 8, QBLK), axis=0)
        inner += jnp.sum(d.reshape(kc // 8, 8, QBLK), axis=0)
        return total, inner

    def finish(h, c, inv, inner):
        slot = h % 2
        a = sbuf[slot, c * kc:(c + 1) * kc, :] * inv
        d = a * ((dpbuf[slot, c * kc:(c + 1) * kc, :] - inner) * SCORE_SCALE)
        p_ref[c * kc:(c + 1) * kc, h * QBLK:(h + 1) * QBLK] = a.astype(BF16)
        ds_ref[c * kc:(c + 1) * kc, h * QBLK:(h + 1) * QBLK] = d.astype(BF16)

    peak = None
    for c in range(nc):
        peak = products(0, c, peak)
    for h in range(heads):
        m = jnp.max(peak, axis=0, keepdims=True)
        total = jnp.zeros((8, QBLK), F32)
        inner = jnp.zeros((8, QBLK), F32)
        peak = None
        for c in range(nc):
            total, inner = weigh(h, c, m, total, inner)
        total = jnp.sum(total, axis=0, keepdims=True)
        inner = jnp.sum(inner, axis=0, keepdims=True)
        inv = 1.0 / total
        inner = inner * inv
        for c in range(nc):
            finish(h, c, inv, inner)
            if h + 1 < heads:
                peak = products(h + 1, c, peak)
    part(heads, reps, rows, ds_ref, p_ref, keys // 2, qbuf, gbuf, far_out)


def part(heads, reps, rows, ds_ref, p_ref, base, qbuf, gbuf, out_ref):
    for r in range(reps):
        at = base + r * rows
        ds = ds_ref[at:at + rows, :]
        p = p_ref[at:at + rows, :]
        kp = lax.dot_general(ds, qbuf[...], NN, preferred_element_type=F32)
        vp = lax.dot_general(p, gbuf[...], NN, preferred_element_type=F32)
        out_ref[:, r * DK:r * DK + DL] = (kp[:, :DL] + vp).astype(BF16)
        out_ref[:, r * DK + DL:(r + 1) * DK] = kp[:, DL:].astype(BF16)


def part_kernel(heads, reps, ds_ref, p_ref, qbuf, gbuf, near_out):
    part(heads, reps, near_out.shape[0], ds_ref, p_ref, 0, qbuf, gbuf, near_out)


def query_kernel(heads, reps, near_ref, far_ref, ds_ref, ready_ref, dq_ref, ktbuf):
    rows = near_ref.shape[0]
    for half, ref in enumerate((near_ref, far_ref)):
        for r in range(reps):
            at = (half * reps + r) * rows
            ktbuf[:, at:at + rows] = ref[:, r * DK:(r + 1) * DK].T
    for h in range(heads):
        dqt = lax.dot_general(ktbuf[...], ds_ref[:, h * QBLK:(h + 1) * QBLK], NN, preferred_element_type=F32)
        dq_ref[:, h * DK:(h + 1) * DK] = dqt.T.astype(BF16)


VM = pl.BlockSpec(memory_space=pltpu.VMEM)


def attend_scores(near, far, q, g):
    rows = near.shape[0]
    reps = near.shape[1] // DK
    heads = q.shape[1] // DK
    keys = 2 * rows * reps
    return pl.pallas_call(
        functools.partial(scores_kernel, heads, reps),
        out_shape=(
            jax.ShapeDtypeStruct((keys, heads * QBLK), BF16),
            jax.ShapeDtypeStruct((keys, heads * QBLK), BF16),
            jax.ShapeDtypeStruct(far.shape, BF16),
            jax.ShapeDtypeStruct((heads * QBLK, DK), BF16),
            jax.ShapeDtypeStruct((heads * QBLK, DL), BF16),
        ),
        in_specs=[VM] * 4,
        out_specs=(VM,) * 5,
        scratch_shapes=[
            pltpu.VMEM((keys, DK), BF16),
            pltpu.VMEM((2, keys, QBLK), F32),
            pltpu.VMEM((2, keys, QBLK), F32),
        ],
        compiler_params=pltpu.CompilerParams(vmem_limit_bytes=30 * 1024 * 1024),
        cost_estimate=pl.CostEstimate(flops=7 * keys * heads * QBLK * DK, bytes_accessed=16 * near.size, transcendentals=keys * heads * QBLK),
        name="attend_scores",
    )(near, far, q, g)


def attend_part(ds, p, qs, gs, shape):
    heads = ds.shape[1] // QBLK
    return pl.pallas_call(
        functools.partial(part_kernel, heads, shape[1] // DK),
        out_shape=jax.ShapeDtypeStruct(shape, BF16),
        in_specs=[VM] * 4,
        out_specs=VM,
        compiler_params=pltpu.CompilerParams(vmem_limit_bytes=20 * 1024 * 1024),
        cost_estimate=pl.CostEstimate(flops=4 * ds.shape[0] // 2 * ds.shape[1] * DK, bytes_accessed=4 * ds.size, transcendentals=0),
        name="attend_part",
    )(ds, p, qs, gs)


def attend_query(near, far, ds, ready):
    heads = ds.shape[1] // QBLK
    reps = near.shape[1] // DK
    return pl.pallas_call(
        functools.partial(query_kernel, heads, reps),
        out_shape=jax.ShapeDtypeStruct((QBLK, heads * DK), BF16),
        in_specs=[VM] * 3 + [pl.BlockSpec(memory_space=pl.ANY)],
        out_specs=VM,
        scratch_shapes=[pltpu.VMEM((DK, ds.shape[0]), BF16)],
        compiler_params=pltpu.CompilerParams(vmem_limit_bytes=20 * 1024 * 1024),
        cost_estimate=pl.CostEstimate(flops=2 * ds.size * DK, bytes_accessed=4 * ds.size, transcendentals=0),
        name="attend_query",
    )(near, far, ds, ready)


def serve_kernel(place, picks_ref, cache_ref, out_ref, sums_ref):
    shards, capacity, width = out_ref.shape
    blocks = cache_ref.shape[0]
    asking = shards // 2
    slots = asking * capacity
    per = picks_ref.shape[1]
    total = asking * per
    rows = [picks_ref[pl.ds(2 * z + place[1], 1), :] for z in range(asking)]
    picks = jnp.concatenate(rows, axis=1)
    mine = (picks // blocks) == place[0]
    within = picks % blocks
    first = lax.broadcasted_iota(jnp.int32, (total, total), 0)
    second = lax.broadcasted_iota(jnp.int32, (total, total), 1)
    before = ((first // per == second // per) & (first < second)).astype(BF16)
    marks = jnp.broadcast_to(mine.astype(F32), (8, total)).astype(BF16)
    rank = lax.dot_general(marks, before, NN, preferred_element_type=F32)[:1].astype(jnp.int32)
    slot = lax.broadcasted_iota(jnp.int32, (slots, total), 0)
    asker = lax.broadcasted_iota(jnp.int32, (slots, total), 1) // per
    spot = jnp.where(mine, rank, capacity)
    left = ((slot // capacity == asker) & (slot % capacity == spot)).astype(BF16)
    block = lax.broadcasted_iota(jnp.int32, (blocks, total), 0)
    right = (block == within).astype(BF16)
    chosen = lax.dot_general(left, right, NT, preferred_element_type=F32).astype(BF16)
    sums_ref[...] = lax.dot_general(right, left, NT, preferred_element_type=F32).astype(BF16)
    served = lax.dot_general(chosen, cache_ref[...], NN, preferred_element_type=F32).astype(BF16)
    for z in range(asking):
        part = served[z * capacity:(z + 1) * capacity]
        out_ref[2 * z] = part[:, :width]
        out_ref[2 * z + 1] = part[:, width:]


def serve(place, picks, cache, groups):
    blocks, whole = cache.shape
    shards, per = picks.shape
    width = whole // groups
    capacity = 2 * per // shards
    return pl.pallas_call(
        serve_kernel,
        out_shape=(
            jax.ShapeDtypeStruct((shards, capacity, width), BF16),
            jax.ShapeDtypeStruct((blocks, shards // 2 * capacity), BF16),
        ),
        grid_spec=pltpu.PrefetchScalarGridSpec(
            num_scalar_prefetch=1,
            grid=(1,),
            in_specs=[
                pl.BlockSpec(picks.shape, lambda i, place: (0, 0)),
                pl.BlockSpec((blocks, 2 * width), lambda i, place: (0, place[2])),
            ],
            out_specs=(
                pl.BlockSpec((shards, capacity, width), lambda i, place: (0, 0, 0)),
                pl.BlockSpec((blocks, shards // 2 * capacity), lambda i, place: (0, 0)),
            ),
        ),
        compiler_params=pltpu.CompilerParams(vmem_limit_bytes=58 * 1024 * 1024),
        name="serve",
    )(place, picks, cache)


def compact_kernel(
    block_count, copies, place, picks_ref, recv_ref, first_ready, second_ready, out_ref, spot_ref
):
    shards, capacity, width = recv_ref.shape
    slots = shards * capacity
    per = picks_ref.shape[1]
    picks = picks_ref[pl.ds(place[3], 1), :]
    holder = picks // block_count
    first = lax.broadcasted_iota(jnp.int32, (per, per), 0)
    second = lax.broadcasted_iota(jnp.int32, (per, per), 1)
    shard = lax.broadcasted_iota(jnp.int32, (shards, per), 0)
    held = shard == holder
    before = (first < second).astype(BF16)
    counts = lax.dot_general(held.astype(BF16), before, NN, preferred_element_type=F32)
    rank = jnp.sum(jnp.where(held, counts, 0.0), axis=0, keepdims=True).astype(jnp.int32)
    slot = lax.broadcasted_iota(jnp.int32, (slots, per), 0)
    spots = (slot == holder * capacity + rank).astype(BF16)
    spot_ref[...] = spots
    recv = jnp.concatenate([recv_ref[c] for c in range(shards)], axis=0)
    picked = lax.dot_general(spots, recv, TN, preferred_element_type=F32).astype(BF16)
    for e in range(copies):
        out_ref[e * per:(e + 1) * per, :] = picked


def compact(place, picks, recv, ready, block_count, copies):
    per = picks.shape[1]
    shards, capacity, width = recv.shape
    vm = pl.BlockSpec(memory_space=pltpu.VMEM)
    return pl.pallas_call(
        functools.partial(compact_kernel, block_count, copies),
        out_shape=(
            jax.ShapeDtypeStruct((copies * per, width), BF16),
            jax.ShapeDtypeStruct((shards * capacity, per), BF16),
        ),
        in_specs=[pl.BlockSpec(memory_space=pltpu.SMEM), vm, vm] + [pl.BlockSpec(memory_space=pl.ANY)] * 2,
        out_specs=(vm, vm),
        compiler_params=pltpu.CompilerParams(vmem_limit_bytes=32 * 1024 * 1024),
        name="compact",
    )(place, picks, recv, *ready)


def pair_kernel(own_ref, other_ref, out_ref):
    out_ref[...] = (own_ref[...].astype(F32) + other_ref[...].astype(F32)).astype(BF16)


def pair_sum(own, other):
    vm = pl.BlockSpec(memory_space=pltpu.VMEM)
    return pl.pallas_call(
        pair_kernel,
        out_shape=jax.ShapeDtypeStruct(own.shape, BF16),
        in_specs=[vm, vm],
        out_specs=vm,
        compiler_params=pltpu.CompilerParams(vmem_limit_bytes=32 * 1024 * 1024),
        name="pair_sum",
    )(own, other)


def fold_kernel(part_ref, spot_ref, held_ref, out_ref, same_ref):
    shards, capacity, width = out_ref.shape
    per = spot_ref.shape[1]
    total = part_ref[:per, :].astype(F32)
    for e in range(1, part_ref.shape[0] // per):
        total += part_ref[e * per:(e + 1) * per, :].astype(F32)
    placed = lax.dot_general(
        spot_ref[...], total.astype(BF16), NN, preferred_element_type=F32
    ).astype(BF16)
    for c in range(shards):
        out_ref[c] = placed[c * capacity:(c + 1) * capacity]


def fold(parts, spots, held, shards):
    width = parts.shape[1]
    vm = pl.BlockSpec(memory_space=pltpu.VMEM)
    return pl.pallas_call(
        fold_kernel,
        out_shape=(
            jax.ShapeDtypeStruct((shards, spots.shape[0] // shards, width), BF16),
            jax.ShapeDtypeStruct(held.shape, held.dtype),
        ),
        in_specs=[vm, vm, pl.BlockSpec(memory_space=pl.ANY)],
        out_specs=(vm, pl.BlockSpec(memory_space=pl.ANY)),
        input_output_aliases={2: 1},
        compiler_params=pltpu.CompilerParams(vmem_limit_bytes=32 * 1024 * 1024),
        name="fold",
    )(parts, spots, held)


def collect_kernel(recv_ref, sums_ref, out_ref):
    shards, capacity, width = recv_ref.shape
    size = out_ref.shape[1]
    for k in range(2):
        recv = jnp.concatenate([recv_ref[2 * z + k] for z in range(shards // 2)], axis=0)
        total = lax.dot_general(sums_ref[...], recv, NN, preferred_element_type=F32).astype(BF16)
        for e in range(out_ref.shape[0]):
            out_ref[e, :, k * width:(k + 1) * width] = total[e * size:(e + 1) * size]


def collect(recv, sums, groups):
    width = recv.shape[2]
    vm = pl.BlockSpec(memory_space=pltpu.VMEM)
    return pl.pallas_call(
        collect_kernel,
        out_shape=jax.ShapeDtypeStruct((groups, sums.shape[0] // groups, 2 * width), BF16),
        in_specs=[vm, vm],
        out_specs=vm,
        compiler_params=pltpu.CompilerParams(vmem_limit_bytes=32 * 1024 * 1024),
        name="collect",
    )(recv, sums)


def settle_kernel(columns, recv_ref, moved_ref, out_ref, query_ref, sem):
    copy = pltpu.make_async_copy(moved_ref, query_ref, sem)
    copy.start()
    width = recv_ref.shape[2]
    for u in range(recv_ref.shape[0] // 2):
        y, half = u // (columns // 2), u % (columns // 2)
        first = y * columns + 2 * half
        both = recv_ref[first].astype(F32) + recv_ref[first + 1].astype(F32)
        out_ref[:, u * width:(u + 1) * width] = both.astype(BF16)
    copy.wait()


def settle(recv, moved, columns):
    groups, rows, width = recv.shape
    vm = pl.BlockSpec(memory_space=pltpu.VMEM)
    hbm = pl.BlockSpec(memory_space=pl.ANY)
    return pl.pallas_call(
        functools.partial(settle_kernel, columns),
        out_shape=(
            jax.ShapeDtypeStruct((rows, groups // 2 * width), BF16),
            jax.ShapeDtypeStruct(moved.shape, BF16),
        ),
        in_specs=[vm, hbm],
        out_specs=(vm, hbm),
        scratch_shapes=[pltpu.SemaphoreType.DMA],
        compiler_params=pltpu.CompilerParams(vmem_limit_bytes=32 * 1024 * 1024),
        name="settle",
    )(recv, moved)


COLUMNS = 4


def colour(group):
    return (group // COLUMNS + group % COLUMNS) % 2


def on_device(queries, latent_cache, block_picks, out_grad):
    shards = lax.axis_size("ctx")
    groups = lax.axis_size("grp")
    block_count = latent_cache.shape[0]
    ctx = lax.axis_index("ctx")
    grp = lax.axis_index("grp")
    mark = colour(grp)
    place = jnp.stack([ctx, mark, grp // 2, ctx // 2 * 2 + mark]).astype(jnp.int32)
    swap = []
    for c in range(shards):
        for e in range(groups):
            moved = c % 2 != colour(e)
            swap.append((c * groups + e, (c ^ 1) * groups + (e ^ 1) if moved else c * groups + e))
    sides = [[e for e in range(groups) if colour(e) == side] for side in range(2)]
    cores = [(c, c ^ 1) for c in range(shards)]
    moved_queries = lax.ppermute(queries, ("ctx", "grp"), swap)
    moved_grad = lax.ppermute(out_grad, ("ctx", "grp"), swap)
    spread = lax.broadcasted_iota(jnp.int32, (shards, block_picks.shape[1]), 0) == ctx
    every = lax.psum(jnp.where(spread, block_picks, 0), "ctx")
    served, sums = serve(place, every, latent_cache, groups)
    fetched = lax.all_to_all(served, "ctx", split_axis=0, concat_axis=0, tiled=True)
    picked, spots = compact(
        place, every, fetched, (moved_queries, moved_grad), block_count, groups // 2
    )
    near = lax.all_to_all(
        picked, "grp", split_axis=0, concat_axis=0, tiled=True, axis_index_groups=sides
    )
    far = lax.ppermute(near, "ctx", cores)
    ds, probs, far_part, query_rows, grad_rows = attend_scores(near, far, moved_queries, moved_grad)
    other_part = lax.ppermute(far_part, "ctx", cores)
    near_part = attend_part(ds, probs, query_rows, grad_rows, near.shape)
    chip_part = pair_sum(near_part, other_part)
    parts = lax.all_to_all(
        chip_part, "grp", split_axis=0, concat_axis=0, tiled=True, axis_index_groups=sides
    )
    part_query_grad = attend_query(near, far, ds, chip_part)
    placed, held_query_grad = fold(parts, spots, part_query_grad, shards)
    moved_query_grad = lax.ppermute(held_query_grad, ("ctx", "grp"), swap)
    returned = lax.all_to_all(placed, "ctx", split_axis=0, concat_axis=0, tiled=True)
    owned = collect(returned, sums, groups)
    final = lax.all_to_all(owned, "grp", split_axis=0, concat_axis=0, tiled=True)
    latent_grad, query_grad = settle(final, moved_query_grad, COLUMNS)
    return (query_grad, latent_grad)


def solution(mesh):
    placed = (P("ctx", "grp"), P("ctx", None), P("ctx", None), P("ctx", "grp"))
    return jax.shard_map(
        on_device,
        mesh=mesh,
        in_specs=placed,
        out_specs=(P("ctx", "grp"), P(("ctx", "grp"), None)),
        check_vma=False,
    )
```

```python
import functools
import jax
import jax.numpy as jnp
from jax import lax
from jax.experimental import pallas as pl
from jax.experimental.pallas import tpu as pltpu
from jax.sharding import PartitionSpec as P

DL = 512
DR = 64
QBLK = 256
DK = 576
SCORE_SCALE = 192.0 ** (-0.5)
LOG2E = 1.4426950408889634
F32 = jnp.float32
BF16 = jnp.bfloat16
NT = (((1,), (1,)), ((), ()))
NN = (((1,), (0,)), ((), ()))
TN = (((0,), (0,)), ((), ()))


def near_kernel(heads, reps, near_ref, q_ref, g_ref, s_ref, dp_ref, peak_ref, qbuf, gbuf, kbuf):
    rows = near_ref.shape[0]
    for r in range(reps):
        kbuf[r * rows:(r + 1) * rows, :] = near_ref[:, r * DK:(r + 1) * DK]
    for h in range(heads):
        qbuf[h * QBLK:(h + 1) * QBLK, :] = q_ref[:, h * DK:(h + 1) * DK]
        gbuf[h * QBLK:(h + 1) * QBLK, :] = g_ref[:, h * DL:(h + 1) * DL]
    for h in range(heads):
        at = slice(h * QBLK, (h + 1) * QBLK)
        s = lax.dot_general(kbuf[...], qbuf[at, :], NT, preferred_element_type=F32)
        s_ref[:, at] = s
        dp_ref[:, at] = lax.dot_general(
            kbuf[:, :DL], gbuf[at, :], NT, preferred_element_type=F32
        )
        peak_ref[:, at] = jnp.max(s.reshape(s.shape[0] // 8, 8, QBLK), axis=0)


def scores_kernel(heads, reps, far_ref, s_ref, dp_ref, peak_ref, qbuf, gbuf, ds_ref, p_ref, far_out,
                  kbuf, sbuf, dpbuf, wbuf, pbuf):
    rows = far_ref.shape[0]
    keys = rows * reps
    for r in range(reps):
        kbuf[r * rows:(r + 1) * rows, :] = far_ref[:, r * DK:(r + 1) * DK]
    kc = 256
    nc = keys // kc
    factor = SCORE_SCALE * LOG2E

    def products(h, c, peak):
        at = slice(h * QBLK, (h + 1) * QBLK)
        to = slice(c * kc, (c + 1) * kc)
        s = lax.dot_general(kbuf[to, :], qbuf[at, :], NT, preferred_element_type=F32)
        sbuf[h % 2, to, :] = s
        dpbuf[h % 2, to, :] = lax.dot_general(
            kbuf[to, :DL], gbuf[at, :], NT, preferred_element_type=F32
        )
        return jnp.maximum(peak, jnp.max(s.reshape(kc // 8, 8, QBLK), axis=0))

    def held(h, c):
        at = slice(h * QBLK, (h + 1) * QBLK)
        if c < nc:
            to = slice(c * kc, (c + 1) * kc)
            return s_ref[to, at], dp_ref[to, at]
        to = slice((c - nc) * kc, (c - nc + 1) * kc)
        return sbuf[h % 2, to, :], dpbuf[h % 2, to, :]

    def peak_of(h):
        return peak_ref[:, h * QBLK:(h + 1) * QBLK]

    peak = peak_of(0)
    for c in range(nc):
        peak = products(0, c, peak)
    for h in range(heads):
        at = slice(h * QBLK, (h + 1) * QBLK)
        m = jnp.max(peak, axis=0, keepdims=True)
        total = jnp.zeros((8, QBLK), F32)
        inner = jnp.zeros((8, QBLK), F32)
        for c in range(2 * nc):
            s, dp = held(h, c)
            w = jnp.exp2((s - m) * factor)
            wbuf[c * kc:(c + 1) * kc, :] = w
            total += jnp.sum(w.reshape(kc // 8, 8, QBLK), axis=0)
            inner += jnp.sum((w * dp).reshape(kc // 8, 8, QBLK), axis=0)
        inv = 1.0 / jnp.sum(total, axis=0, keepdims=True)
        inner = jnp.sum(inner, axis=0, keepdims=True) * inv
        if h + 1 < heads:
            peak = peak_of(h + 1)
        for c in range(2 * nc):
            dp = held(h, c)[1]
            a = wbuf[c * kc:(c + 1) * kc, :] * inv
            d = a * ((dp - inner) * SCORE_SCALE)
            if c < nc:
                p_ref[c * kc:(c + 1) * kc, at] = a.astype(BF16)
            else:
                pbuf[(c - nc) * kc:(c - nc + 1) * kc, at] = a.astype(BF16)
            ds_ref[c * kc:(c + 1) * kc, at] = d.astype(BF16)
            if h + 1 < heads and c % 2 == 1:
                peak = products(h + 1, c // 2, peak)
    part(heads, reps, rows, ds_ref, keys, pbuf, qbuf, gbuf, far_out)


def part(heads, reps, rows, ds_ref, base, p_ref, qbuf, gbuf, out_ref):
    for r in range(reps):
        ds = ds_ref[base + r * rows:base + (r + 1) * rows, :]
        p = p_ref[r * rows:(r + 1) * rows, :]
        kp = lax.dot_general(ds, qbuf[...], NN, preferred_element_type=F32)
        vp = lax.dot_general(p, gbuf[...], NN, preferred_element_type=F32)
        out_ref[:, r * DK:r * DK + DL] = (kp[:, :DL] + vp).astype(BF16)
        out_ref[:, r * DK + DL:(r + 1) * DK] = kp[:, DL:].astype(BF16)


def part_kernel(heads, reps, ds_ref, p_ref, qbuf, gbuf, near_out):
    part(heads, reps, near_out.shape[0], ds_ref, 0, p_ref, qbuf, gbuf, near_out)


def query_kernel(heads, reps, near_ref, far_ref, ds_ref, ready_ref, dq_ref, ktbuf):
    rows = near_ref.shape[0]
    for half, ref in enumerate((near_ref, far_ref)):
        for r in range(reps):
            at = (half * reps + r) * rows
            ktbuf[:, at:at + rows] = ref[:, r * DK:(r + 1) * DK].T
    for h in range(heads):
        dqt = lax.dot_general(ktbuf[...], ds_ref[:, h * QBLK:(h + 1) * QBLK], NN, preferred_element_type=F32)
        dq_ref[:, h * DK:(h + 1) * DK] = dqt.T.astype(BF16)


VM = pl.BlockSpec(memory_space=pltpu.VMEM)


def attend_near(near, q, g):
    rows = near.shape[0]
    reps = near.shape[1] // DK
    heads = q.shape[1] // DK
    keys = rows * reps
    wide = heads * QBLK
    return pl.pallas_call(
        functools.partial(near_kernel, heads, reps),
        out_shape=(
            jax.ShapeDtypeStruct((keys, wide), F32),
            jax.ShapeDtypeStruct((keys, wide), F32),
            jax.ShapeDtypeStruct((8, wide), F32),
            jax.ShapeDtypeStruct((wide, DK), BF16),
            jax.ShapeDtypeStruct((wide, DL), BF16),
        ),
        in_specs=[VM] * 3,
        out_specs=(VM,) * 5,
        scratch_shapes=[pltpu.VMEM((keys, DK), BF16)],
        compiler_params=pltpu.CompilerParams(vmem_limit_bytes=20 * 1024 * 1024),
        cost_estimate=pl.CostEstimate(
            flops=4 * keys * wide * DK, bytes_accessed=16 * near.size, transcendentals=0
        ),
        name="attend_near",
    )(near, q, g)


def attend_scores(far, scores, dprobs, peaks, qs, gs):
    rows = far.shape[0]
    reps = far.shape[1] // DK
    heads = qs.shape[0] // QBLK
    keys = rows * reps
    wide = heads * QBLK
    return pl.pallas_call(
        functools.partial(scores_kernel, heads, reps),
        out_shape=(
            jax.ShapeDtypeStruct((2 * keys, wide), BF16),
            jax.ShapeDtypeStruct((keys, wide), BF16),
            jax.ShapeDtypeStruct(far.shape, BF16),
        ),
        in_specs=[VM] * 6,
        out_specs=(VM,) * 3,
        scratch_shapes=[
            pltpu.VMEM((keys, DK), BF16),
            pltpu.VMEM((2, keys, QBLK), F32),
            pltpu.VMEM((2, keys, QBLK), F32),
            pltpu.VMEM((2 * keys, QBLK), F32),
            pltpu.VMEM((keys, wide), BF16),
        ],
        compiler_params=pltpu.CompilerParams(vmem_limit_bytes=34 * 1024 * 1024),
        cost_estimate=pl.CostEstimate(
            flops=6 * keys * wide * DK, bytes_accessed=16 * far.size, transcendentals=keys * wide
        ),
        name="attend_scores",
    )(far, scores, dprobs, peaks, qs, gs)


def attend_part(ds, p, qs, gs, shape):
    heads = ds.shape[1] // QBLK
    return pl.pallas_call(
        functools.partial(part_kernel, heads, shape[1] // DK),
        out_shape=jax.ShapeDtypeStruct(shape, BF16),
        in_specs=[VM] * 4,
        out_specs=VM,
        compiler_params=pltpu.CompilerParams(vmem_limit_bytes=16 * 1024 * 1024),
        cost_estimate=pl.CostEstimate(flops=4 * ds.shape[0] // 2 * ds.shape[1] * DK, bytes_accessed=4 * ds.size, transcendentals=0),
        name="attend_part",
    )(ds, p, qs, gs)


def attend_query(near, far, ds, ready):
    heads = ds.shape[1] // QBLK
    reps = near.shape[1] // DK
    return pl.pallas_call(
        functools.partial(query_kernel, heads, reps),
        out_shape=jax.ShapeDtypeStruct((QBLK, heads * DK), BF16),
        in_specs=[VM] * 3 + [pl.BlockSpec(memory_space=pl.ANY)],
        out_specs=VM,
        scratch_shapes=[pltpu.VMEM((DK, ds.shape[0]), BF16)],
        compiler_params=pltpu.CompilerParams(vmem_limit_bytes=14 * 1024 * 1024),
        cost_estimate=pl.CostEstimate(flops=2 * ds.size * DK, bytes_accessed=4 * ds.size, transcendentals=0),
        name="attend_query",
    )(near, far, ds, ready)


def serve_kernel(picks_ref, cache_ref, out_ref, sums_ref, slice_ref, sem):
    shards, capacity, width = out_ref.shape
    blocks = cache_ref.shape[0]
    me = lax.axis_index("ctx")
    group = lax.axis_index("grp")
    start = pl.multiple_of((group // 2) * (2 * width), 128)
    copy = pltpu.make_async_copy(cache_ref.at[:, pl.ds(start, 2 * width)], slice_ref, sem)
    copy.start()
    asking = shards // 2
    slots = asking * capacity
    per = picks_ref.shape[1]
    total = asking * per
    mark = colour(group)
    rows = [picks_ref[pl.ds(2 * z + mark, 1), :] for z in range(asking)]
    picks = jnp.concatenate(rows, axis=1)
    mine = (picks // blocks) == me
    within = picks % blocks
    first = lax.broadcasted_iota(jnp.int32, (total, total), 0)
    second = lax.broadcasted_iota(jnp.int32, (total, total), 1)
    before = ((first // per == second // per) & (first < second)).astype(BF16)
    marks = jnp.broadcast_to(mine.astype(F32), (8, total)).astype(BF16)
    rank = lax.dot_general(marks, before, NN, preferred_element_type=F32)[:1].astype(jnp.int32)
    slot = lax.broadcasted_iota(jnp.int32, (slots, total), 0)
    asker = lax.broadcasted_iota(jnp.int32, (slots, total), 1) // per
    spot = jnp.where(mine, rank, capacity)
    left = ((slot // capacity == asker) & (slot % capacity == spot)).astype(BF16)
    block = lax.broadcasted_iota(jnp.int32, (blocks, total), 0)
    right = (block == within).astype(BF16)
    chosen = lax.dot_general(left, right, NT, preferred_element_type=F32).astype(BF16)
    sums_ref[...] = lax.dot_general(right, left, NT, preferred_element_type=F32).astype(BF16)
    copy.wait()
    served = lax.dot_general(chosen, slice_ref[...], NN, preferred_element_type=F32).astype(BF16)
    for z in range(asking):
        part = served[z * capacity:(z + 1) * capacity]
        out_ref[2 * z] = part[:, :width]
        out_ref[2 * z + 1] = part[:, width:]


def serve(picks, cache, groups):
    blocks, whole = cache.shape
    shards, per = picks.shape
    width = whole // groups
    capacity = 2 * per // shards
    return pl.pallas_call(
        serve_kernel,
        out_shape=(
            jax.ShapeDtypeStruct((shards, capacity, width), BF16),
            jax.ShapeDtypeStruct((blocks, shards // 2 * capacity), BF16),
        ),
        in_specs=[VM, pl.BlockSpec(memory_space=pl.ANY)],
        out_specs=(VM, VM),
        scratch_shapes=[pltpu.VMEM((blocks, 2 * width), BF16), pltpu.SemaphoreType.DMA],
        compiler_params=pltpu.CompilerParams(vmem_limit_bytes=58 * 1024 * 1024),
        name="serve",
    )(picks, cache)


def compact_kernel(
    block_count, copies, picks_ref, recv_ref, first_ready, second_ready, out_ref, spot_ref
):
    shards, capacity, width = recv_ref.shape
    slots = shards * capacity
    per = picks_ref.shape[1]
    row = lax.axis_index("ctx") // 2 * 2 + colour(lax.axis_index("grp"))
    picks = picks_ref[pl.ds(row, 1), :]
    holder = picks // block_count
    first = lax.broadcasted_iota(jnp.int32, (per, per), 0)
    second = lax.broadcasted_iota(jnp.int32, (per, per), 1)
    shard = lax.broadcasted_iota(jnp.int32, (shards, per), 0)
    held = shard == holder
    before = (first < second).astype(BF16)
    counts = lax.dot_general(held.astype(BF16), before, NN, preferred_element_type=F32)
    rank = jnp.sum(jnp.where(held, counts, 0.0), axis=0, keepdims=True).astype(jnp.int32)
    slot = lax.broadcasted_iota(jnp.int32, (slots, per), 0)
    spots = (slot == holder * capacity + rank).astype(BF16)
    spot_ref[...] = spots
    recv = jnp.concatenate([recv_ref[c] for c in range(shards)], axis=0)
    picked = lax.dot_general(spots, recv, TN, preferred_element_type=F32).astype(BF16)
    for e in range(copies):
        out_ref[e * per:(e + 1) * per, :] = picked


def compact(picks, recv, ready, block_count, copies):
    per = picks.shape[1]
    shards, capacity, width = recv.shape
    vm = pl.BlockSpec(memory_space=pltpu.VMEM)
    return pl.pallas_call(
        functools.partial(compact_kernel, block_count, copies),
        out_shape=(
            jax.ShapeDtypeStruct((copies * per, width), BF16),
            jax.ShapeDtypeStruct((shards * capacity, per), BF16),
        ),
        in_specs=[vm, vm] + [pl.BlockSpec(memory_space=pl.ANY)] * 2,
        out_specs=(vm, vm),
        compiler_params=pltpu.CompilerParams(vmem_limit_bytes=8 * 1024 * 1024),
        name="compact",
    )(picks, recv, *ready)


def pair_kernel(own_ref, other_ref, out_ref):
    out_ref[...] = (own_ref[...].astype(F32) + other_ref[...].astype(F32)).astype(BF16)


def pair_sum(own, other):
    vm = pl.BlockSpec(memory_space=pltpu.VMEM)
    return pl.pallas_call(
        pair_kernel,
        out_shape=jax.ShapeDtypeStruct(own.shape, BF16),
        in_specs=[vm, vm],
        out_specs=vm,
        compiler_params=pltpu.CompilerParams(vmem_limit_bytes=8 * 1024 * 1024),
        name="pair_sum",
    )(own, other)


def fold_kernel(part_ref, spot_ref, out_ref):
    shards, capacity, width = out_ref.shape
    per = spot_ref.shape[1]
    total = part_ref[:per, :].astype(F32)
    for e in range(1, part_ref.shape[0] // per):
        total += part_ref[e * per:(e + 1) * per, :].astype(F32)
    placed = lax.dot_general(
        spot_ref[...], total.astype(BF16), NN, preferred_element_type=F32
    ).astype(BF16)
    for c in range(shards):
        out_ref[c] = placed[c * capacity:(c + 1) * capacity]


def fold(parts, spots, shards):
    width = parts.shape[1]
    vm = pl.BlockSpec(memory_space=pltpu.VMEM)
    return pl.pallas_call(
        fold_kernel,
        out_shape=jax.ShapeDtypeStruct((shards, spots.shape[0] // shards, width), BF16),
        in_specs=[vm, vm],
        out_specs=vm,
        compiler_params=pltpu.CompilerParams(vmem_limit_bytes=8 * 1024 * 1024),
        name="fold",
    )(parts, spots)


def collect_kernel(recv_ref, sums_ref, out_ref):
    shards, capacity, width = recv_ref.shape
    size = out_ref.shape[1]
    for k in range(2):
        recv = jnp.concatenate([recv_ref[2 * z + k] for z in range(shards // 2)], axis=0)
        total = lax.dot_general(sums_ref[...], recv, NN, preferred_element_type=F32).astype(BF16)
        for e in range(out_ref.shape[0]):
            out_ref[e, :, k * width:(k + 1) * width] = total[e * size:(e + 1) * size]


def collect(recv, sums, groups):
    width = recv.shape[2]
    vm = pl.BlockSpec(memory_space=pltpu.VMEM)
    return pl.pallas_call(
        collect_kernel,
        out_shape=jax.ShapeDtypeStruct((groups, sums.shape[0] // groups, 2 * width), BF16),
        in_specs=[vm, vm],
        out_specs=vm,
        compiler_params=pltpu.CompilerParams(vmem_limit_bytes=8 * 1024 * 1024),
        name="collect",
    )(recv, sums)


def settle_kernel(columns, recv_ref, moved_ref, out_ref, query_ref, sem):
    copy = pltpu.make_async_copy(moved_ref, query_ref, sem)
    copy.start()
    width = recv_ref.shape[2]
    for u in range(recv_ref.shape[0] // 2):
        y, half = u // (columns // 2), u % (columns // 2)
        first = y * columns + 2 * half
        both = recv_ref[first].astype(F32) + recv_ref[first + 1].astype(F32)
        out_ref[:, u * width:(u + 1) * width] = both.astype(BF16)
    copy.wait()


def settle(recv, moved, columns):
    groups, rows, width = recv.shape
    vm = pl.BlockSpec(memory_space=pltpu.VMEM)
    hbm = pl.BlockSpec(memory_space=pl.ANY)
    return pl.pallas_call(
        functools.partial(settle_kernel, columns),
        out_shape=(
            jax.ShapeDtypeStruct((rows, groups // 2 * width), BF16),
            jax.ShapeDtypeStruct(moved.shape, BF16),
        ),
        in_specs=[vm, hbm],
        out_specs=(vm, hbm),
        scratch_shapes=[pltpu.SemaphoreType.DMA],
        compiler_params=pltpu.CompilerParams(vmem_limit_bytes=8 * 1024 * 1024),
        name="settle",
    )(recv, moved)


COLUMNS = 4


def colour(group):
    return (group // COLUMNS + group % COLUMNS) % 2


def on_device(queries, latent_cache, block_picks, out_grad):
    shards = lax.axis_size("ctx")
    groups = lax.axis_size("grp")
    block_count = latent_cache.shape[0]
    ctx = lax.axis_index("ctx")
    swap = []
    for c in range(shards):
        for e in range(groups):
            moved = c % 2 != colour(e)
            swap.append((c * groups + e, (c ^ 1) * groups + (e ^ 1) if moved else c * groups + e))
    sides = [[e for e in range(groups) if colour(e) == side] for side in range(2)]
    cores = [(c, c ^ 1) for c in range(shards)]
    moved_queries = lax.ppermute(queries, ("ctx", "grp"), swap)
    moved_grad = lax.ppermute(out_grad, ("ctx", "grp"), swap)
    spread = lax.broadcasted_iota(jnp.int32, (shards, block_picks.shape[1]), 0) == ctx
    every = lax.psum(jnp.where(spread, block_picks, 0), "ctx")
    served, sums = serve(every, latent_cache, groups)
    fetched = lax.all_to_all(served, "ctx", split_axis=0, concat_axis=0, tiled=True)
    picked, spots = compact(
        every, fetched, (moved_queries, moved_grad), block_count, groups // 2
    )
    near = lax.all_to_all(
        picked, "grp", split_axis=0, concat_axis=0, tiled=True, axis_index_groups=sides
    )
    far = lax.ppermute(near, "ctx", cores)
    scores, dprobs, peaks, query_rows, grad_rows = attend_near(near, moved_queries, moved_grad)
    ds, probs, far_part = attend_scores(far, scores, dprobs, peaks, query_rows, grad_rows)
    other_part = lax.ppermute(far_part, "ctx", cores)
    near_part = attend_part(ds, probs, query_rows, grad_rows, near.shape)
    chip_part = pair_sum(near_part, other_part)
    parts = lax.all_to_all(
        chip_part, "grp", split_axis=0, concat_axis=0, tiled=True, axis_index_groups=sides
    )
    part_query_grad = attend_query(near, far, ds, chip_part)
    moved_query_grad = lax.ppermute(part_query_grad, ("ctx", "grp"), swap)
    placed = fold(parts, spots, shards)
    returned = lax.all_to_all(placed, "ctx", split_axis=0, concat_axis=0, tiled=True)
    owned = collect(returned, sums, groups)
    final = lax.all_to_all(owned, "grp", split_axis=0, concat_axis=0, tiled=True)
    latent_grad, query_grad = settle(final, moved_query_grad, COLUMNS)
    return (query_grad, latent_grad)


def solution(mesh):
    placed = (P("ctx", "grp"), P("ctx", None), P("ctx", None), P("ctx", "grp"))
    return jax.shard_map(
        on_device,
        mesh=mesh,
        in_specs=placed,
        out_specs=(P("ctx", "grp"), P(("ctx", "grp"), None)),
        check_vma=False,
    )
```

```python
import functools
import jax
import jax.numpy as jnp
from jax import lax
from jax.experimental import pallas as pl
from jax.experimental.pallas import tpu as pltpu
from jax.sharding import PartitionSpec as P

DL = 512
DR = 64
QBLK = 256
DK = 576
SCORE_SCALE = 192.0 ** (-0.5)
LOG2E = 1.4426950408889634
F32 = jnp.float32
BF16 = jnp.bfloat16
NT = (((1,), (1,)), ((), ()))
NN = (((1,), (0,)), ((), ()))
TN = (((0,), (0,)), ((), ()))


def near_kernel(heads, reps, near_ref, q_ref, g_ref, s_ref, dp_ref, peak_ref, qbuf, gbuf, kbuf):
    rows = near_ref.shape[0]
    for r in range(reps):
        kbuf[r * rows:(r + 1) * rows, :] = near_ref[:, r * DK:(r + 1) * DK]
    for h in range(heads):
        qbuf[h * QBLK:(h + 1) * QBLK, :] = q_ref[:, h * DK:(h + 1) * DK]
        gbuf[h * QBLK:(h + 1) * QBLK, :] = g_ref[:, h * DL:(h + 1) * DL]
    for h in range(heads):
        at = slice(h * QBLK, (h + 1) * QBLK)
        s = lax.dot_general(kbuf[...], qbuf[at, :], NT, preferred_element_type=F32)
        s_ref[:, at] = s
        dp_ref[:, at] = lax.dot_general(
            kbuf[:, :DL], gbuf[at, :], NT, preferred_element_type=F32
        )
        peak_ref[:, at] = jnp.max(s.reshape(s.shape[0] // 8, 8, QBLK), axis=0)


def scores_kernel(heads, reps, far_ref, s_ref, dp_ref, peak_ref, qbuf, gbuf, ds_ref, p_ref, far_out,
                  kbuf, sbuf, dpbuf, wbuf, pbuf):
    rows = far_ref.shape[0]
    keys = rows * reps
    for r in range(reps):
        kbuf[r * rows:(r + 1) * rows, :] = far_ref[:, r * DK:(r + 1) * DK]
    kc = 256
    nc = keys // kc
    factor = SCORE_SCALE * LOG2E

    def products(h, c, peak):
        at = slice(h * QBLK, (h + 1) * QBLK)
        to = slice(c * kc, (c + 1) * kc)
        s = lax.dot_general(kbuf[to, :], qbuf[at, :], NT, preferred_element_type=F32)
        sbuf[h % 2, to, :] = s
        dpbuf[h % 2, to, :] = lax.dot_general(
            kbuf[to, :DL], gbuf[at, :], NT, preferred_element_type=F32
        )
        return jnp.maximum(peak, jnp.max(s.reshape(kc // 8, 8, QBLK), axis=0))

    def held(h, c):
        at = slice(h * QBLK, (h + 1) * QBLK)
        if c < nc:
            to = slice(c * kc, (c + 1) * kc)
            return s_ref[to, at], dp_ref[to, at]
        to = slice((c - nc) * kc, (c - nc + 1) * kc)
        return sbuf[h % 2, to, :], dpbuf[h % 2, to, :]

    def peak_of(h):
        return peak_ref[:, h * QBLK:(h + 1) * QBLK]

    peak = peak_of(0)
    for c in range(nc):
        peak = products(0, c, peak)
    for h in range(heads):
        at = slice(h * QBLK, (h + 1) * QBLK)
        m = jnp.max(peak, axis=0, keepdims=True)
        total = jnp.zeros((8, QBLK), F32)
        inner = jnp.zeros((8, QBLK), F32)
        for c in range(2 * nc):
            s, dp = held(h, c)
            w = jnp.exp2((s - m) * factor)
            wbuf[c * kc:(c + 1) * kc, :] = w
            total += jnp.sum(w.reshape(kc // 8, 8, QBLK), axis=0)
            inner += jnp.sum((w * dp).reshape(kc // 8, 8, QBLK), axis=0)
        inv = 1.0 / jnp.sum(total, axis=0, keepdims=True)
        inner = jnp.sum(inner, axis=0, keepdims=True) * inv
        if h + 1 < heads:
            peak = peak_of(h + 1)
        for c in range(2 * nc):
            dp = held(h, c)[1]
            a = wbuf[c * kc:(c + 1) * kc, :] * inv
            d = a * ((dp - inner) * SCORE_SCALE)
            if c < nc:
                p_ref[c * kc:(c + 1) * kc, at] = a.astype(BF16)
            else:
                pbuf[(c - nc) * kc:(c - nc + 1) * kc, at] = a.astype(BF16)
            ds_ref[c * kc:(c + 1) * kc, at] = d.astype(BF16)
            if h + 1 < heads and c % 2 == 1:
                peak = products(h + 1, c // 2, peak)
    part(heads, reps, rows, ds_ref, keys, pbuf, qbuf, gbuf, far_out)


def part(heads, reps, rows, ds_ref, base, p_ref, qbuf, gbuf, out_ref):
    for r in range(reps):
        ds = ds_ref[base + r * rows:base + (r + 1) * rows, :]
        p = p_ref[r * rows:(r + 1) * rows, :]
        kp = lax.dot_general(ds, qbuf[...], NN, preferred_element_type=F32)
        vp = lax.dot_general(p, gbuf[...], NN, preferred_element_type=F32)
        out_ref[:, r * DK:r * DK + DL] = (kp[:, :DL] + vp).astype(BF16)
        out_ref[:, r * DK + DL:(r + 1) * DK] = kp[:, DL:].astype(BF16)


def part_kernel(heads, reps, ds_ref, p_ref, qbuf, gbuf, near_out):
    part(heads, reps, near_out.shape[0], ds_ref, 0, p_ref, qbuf, gbuf, near_out)


def query_kernel(heads, reps, near_ref, far_ref, ds_ref, ready_ref, dq_ref, ktbuf):
    rows = near_ref.shape[0]
    for half, ref in enumerate((near_ref, far_ref)):
        for r in range(reps):
            at = (half * reps + r) * rows
            ktbuf[:, at:at + rows] = ref[:, r * DK:(r + 1) * DK].T
    for h in range(heads):
        dqt = lax.dot_general(ktbuf[...], ds_ref[:, h * QBLK:(h + 1) * QBLK], NN, preferred_element_type=F32)
        dq_ref[:, h * DK:(h + 1) * DK] = dqt.T.astype(BF16)


VM = pl.BlockSpec(memory_space=pltpu.VMEM)


def attend_near(near, q, g):
    rows = near.shape[0]
    reps = near.shape[1] // DK
    heads = q.shape[1] // DK
    keys = rows * reps
    wide = heads * QBLK
    return pl.pallas_call(
        functools.partial(near_kernel, heads, reps),
        out_shape=(
            jax.ShapeDtypeStruct((keys, wide), F32),
            jax.ShapeDtypeStruct((keys, wide), F32),
            jax.ShapeDtypeStruct((8, wide), F32),
            jax.ShapeDtypeStruct((wide, DK), BF16),
            jax.ShapeDtypeStruct((wide, DL), BF16),
        ),
        in_specs=[VM] * 3,
        out_specs=(VM,) * 5,
        scratch_shapes=[pltpu.VMEM((keys, DK), BF16)],
        compiler_params=pltpu.CompilerParams(vmem_limit_bytes=20 * 1024 * 1024),
        cost_estimate=pl.CostEstimate(
            flops=4 * keys * wide * DK, bytes_accessed=16 * near.size, transcendentals=0
        ),
        name="attend_near",
    )(near, q, g)


def attend_scores(far, scores, dprobs, peaks, qs, gs):
    rows = far.shape[0]
    reps = far.shape[1] // DK
    heads = qs.shape[0] // QBLK
    keys = rows * reps
    wide = heads * QBLK
    return pl.pallas_call(
        functools.partial(scores_kernel, heads, reps),
        out_shape=(
            jax.ShapeDtypeStruct((2 * keys, wide), BF16),
            jax.ShapeDtypeStruct((keys, wide), BF16),
            jax.ShapeDtypeStruct(far.shape, BF16),
        ),
        in_specs=[VM] * 6,
        out_specs=(VM,) * 3,
        scratch_shapes=[
            pltpu.VMEM((keys, DK), BF16),
            pltpu.VMEM((2, keys, QBLK), F32),
            pltpu.VMEM((2, keys, QBLK), F32),
            pltpu.VMEM((2 * keys, QBLK), F32),
            pltpu.VMEM((keys, wide), BF16),
        ],
        compiler_params=pltpu.CompilerParams(vmem_limit_bytes=34 * 1024 * 1024),
        cost_estimate=pl.CostEstimate(
            flops=6 * keys * wide * DK, bytes_accessed=16 * far.size, transcendentals=keys * wide
        ),
        name="attend_scores",
    )(far, scores, dprobs, peaks, qs, gs)


def attend_part(ds, p, qs, gs, shape):
    heads = ds.shape[1] // QBLK
    return pl.pallas_call(
        functools.partial(part_kernel, heads, shape[1] // DK),
        out_shape=jax.ShapeDtypeStruct(shape, BF16),
        in_specs=[VM] * 4,
        out_specs=VM,
        compiler_params=pltpu.CompilerParams(vmem_limit_bytes=16 * 1024 * 1024),
        cost_estimate=pl.CostEstimate(flops=4 * ds.shape[0] // 2 * ds.shape[1] * DK, bytes_accessed=4 * ds.size, transcendentals=0),
        name="attend_part",
    )(ds, p, qs, gs)


def attend_query(near, far, ds, ready):
    heads = ds.shape[1] // QBLK
    reps = near.shape[1] // DK
    return pl.pallas_call(
        functools.partial(query_kernel, heads, reps),
        out_shape=jax.ShapeDtypeStruct((QBLK, heads * DK), BF16),
        in_specs=[VM] * 3 + [pl.BlockSpec(memory_space=pl.ANY)],
        out_specs=VM,
        scratch_shapes=[pltpu.VMEM((DK, ds.shape[0]), BF16)],
        compiler_params=pltpu.CompilerParams(vmem_limit_bytes=14 * 1024 * 1024),
        cost_estimate=pl.CostEstimate(flops=2 * ds.size * DK, bytes_accessed=4 * ds.size, transcendentals=0),
        name="attend_query",
    )(near, far, ds, ready)


def shifted(values, size):
    return lax.shift_right_logical(values, size.bit_length() - 1)


def serve_kernel(picks_ref, cache_ref, out_ref, slice_ref, sem):
    shards, capacity, width = out_ref.shape
    blocks = cache_ref.shape[0]
    me = lax.axis_index("ctx")
    group = lax.axis_index("grp")
    start = pl.multiple_of((group // 2) * (2 * width), 128)
    copy = pltpu.make_async_copy(cache_ref.at[:, pl.ds(start, 2 * width)], slice_ref, sem)
    copy.start()
    asking = shards // 2
    slots = asking * capacity
    per = picks_ref.shape[1]
    total = asking * per
    mark = colour(group)
    rows = [picks_ref[pl.ds(2 * z + mark, 1), :] for z in range(asking)]
    picks = jnp.concatenate(rows, axis=0)
    mine = shifted(picks, blocks) == me
    first = lax.broadcasted_iota(jnp.int32, (per, per), 0)
    second = lax.broadcasted_iota(jnp.int32, (per, per), 1)
    before = (first < second).astype(BF16)
    rank = lax.dot_general(mine.astype(BF16), before, NN, preferred_element_type=F32)
    spots = jnp.where(mine, rank.astype(jnp.int32), capacity)
    spot = jnp.concatenate([spots[z:z + 1] for z in range(asking)], axis=1)
    within = jnp.concatenate([rows[z] & (blocks - 1) for z in range(asking)], axis=1)
    slot = lax.broadcasted_iota(jnp.int32, (slots, total), 0)
    asker = shifted(lax.broadcasted_iota(jnp.int32, (slots, total), 1), per)
    left = (slot == asker * capacity + spot) & (spot < capacity)
    block = lax.broadcasted_iota(jnp.int32, (blocks, total), 0)
    right = (block == within).astype(BF16)
    chosen = lax.dot_general(left.astype(BF16), right, NT, preferred_element_type=F32).astype(BF16)
    copy.wait()
    served = lax.dot_general(chosen, slice_ref[...], NN, preferred_element_type=F32).astype(BF16)
    for z in range(asking):
        part = served[z * capacity:(z + 1) * capacity]
        out_ref[2 * z] = part[:, :width]
        out_ref[2 * z + 1] = part[:, width:]


def serve(picks, cache, groups):
    blocks, whole = cache.shape
    shards, per = picks.shape
    width = whole // groups
    capacity = 2 * per // shards
    return pl.pallas_call(
        serve_kernel,
        out_shape=jax.ShapeDtypeStruct((shards, capacity, width), BF16),
        in_specs=[VM, pl.BlockSpec(memory_space=pl.ANY)],
        out_specs=VM,
        scratch_shapes=[pltpu.VMEM((blocks, 2 * width), BF16), pltpu.SemaphoreType.DMA],
        compiler_params=pltpu.CompilerParams(vmem_limit_bytes=58 * 1024 * 1024),
        name="serve",
    )(picks, cache)


def spots_of(picks, shards, capacity, block_count):
    slots = shards * capacity
    per = picks.shape[1]
    holder = shifted(picks, block_count)
    first = lax.broadcasted_iota(jnp.int32, (per, per), 0)
    second = lax.broadcasted_iota(jnp.int32, (per, per), 1)
    shard = lax.broadcasted_iota(jnp.int32, (shards, per), 0)
    held = shard == holder
    before = (first < second).astype(BF16)
    counts = lax.dot_general(held.astype(BF16), before, NN, preferred_element_type=F32)
    rank = jnp.sum(jnp.where(held, counts, 0.0), axis=0, keepdims=True).astype(jnp.int32)
    slot = lax.broadcasted_iota(jnp.int32, (slots, per), 0)
    return (slot == holder * capacity + rank).astype(BF16)


def compact_kernel(block_count, copies, picks_ref, recv_ref, ready_ref, out_ref):
    shards, capacity, width = recv_ref.shape
    per = picks_ref.shape[1]
    row = lax.axis_index("ctx") // 2 * 2 + colour(lax.axis_index("grp"))
    spots = spots_of(picks_ref[pl.ds(row, 1), :], shards, capacity, block_count)
    recv = jnp.concatenate([recv_ref[c] for c in range(shards)], axis=0)
    picked = lax.dot_general(spots, recv, TN, preferred_element_type=F32).astype(BF16)
    for e in range(copies):
        out_ref[e * per:(e + 1) * per, :] = picked


def compact(picks, recv, ready, block_count, copies):
    per = picks.shape[1]
    hold = pl.BlockSpec(memory_space=pl.ANY)
    return pl.pallas_call(
        functools.partial(compact_kernel, block_count, copies),
        out_shape=jax.ShapeDtypeStruct((copies * per, recv.shape[2]), BF16),
        in_specs=[VM, VM, hold],
        out_specs=VM,
        compiler_params=pltpu.CompilerParams(vmem_limit_bytes=8 * 1024 * 1024),
        name="compact",
    )(picks, recv, ready)


def plan_kernel(block_count, picks_ref, ready_ref, sums_ref, spots_ref):
    shards, per = picks_ref.shape
    total = shards * per
    slots = sums_ref.shape[1]
    capacity = slots // shards
    me = lax.axis_index("ctx")
    picks = jnp.concatenate([picks_ref[c:c + 1, :] for c in range(shards)], axis=1)
    mine = (picks // block_count) == me
    within = picks % block_count
    first = lax.broadcasted_iota(jnp.int32, (total, total), 0)
    second = lax.broadcasted_iota(jnp.int32, (total, total), 1)
    before = ((first // per == second // per) & (first < second)).astype(BF16)
    marks = jnp.broadcast_to(mine.astype(F32), (8, total)).astype(BF16)
    rank = lax.dot_general(marks, before, NN, preferred_element_type=F32)[:1].astype(jnp.int32)
    slot = lax.broadcasted_iota(jnp.int32, (slots, total), 0)
    asker = lax.broadcasted_iota(jnp.int32, (slots, total), 1) // per
    spot = jnp.where(mine, rank, capacity)
    left = ((slot // capacity == asker) & (slot % capacity == spot)).astype(BF16)
    block = lax.broadcasted_iota(jnp.int32, (block_count, total), 0)
    right = (block == within).astype(BF16)
    sums_ref[...] = lax.dot_general(right, left, NT, preferred_element_type=F32).astype(BF16)
    for side in range(2):
        row = me // 2 * 2 + side
        spots_ref[side] = spots_of(picks_ref[pl.ds(row, 1), :], shards, capacity, block_count)


def plan(picks, ready, block_count):
    shards, per = picks.shape
    slots = 2 * per
    return pl.pallas_call(
        functools.partial(plan_kernel, block_count),
        out_shape=(
            jax.ShapeDtypeStruct((block_count, slots), BF16),
            jax.ShapeDtypeStruct((2, slots, per), BF16),
        ),
        in_specs=[VM, pl.BlockSpec(memory_space=pl.ANY)],
        out_specs=(VM, VM),
        compiler_params=pltpu.CompilerParams(vmem_limit_bytes=8 * 1024 * 1024),
        cost_estimate=pl.CostEstimate(flops=10**9, bytes_accessed=10**6, transcendentals=0),
        name="plan",
    )(picks, ready)


def pair_kernel(own_ref, other_ref, out_ref):
    groups, per, width = out_ref.shape
    for g in range(groups):
        rows = slice(g // 2 * per, (g // 2 + 1) * per)
        at = slice(colour(g) * width, (colour(g) + 1) * width)
        both = own_ref[rows, at].astype(F32) + other_ref[rows, at].astype(F32)
        out_ref[g] = both.astype(BF16)


def pair_sum(own, other, groups):
    rows, width = own.shape
    return pl.pallas_call(
        pair_kernel,
        out_shape=jax.ShapeDtypeStruct((groups, 2 * rows // groups, width // 2), BF16),
        in_specs=[VM, VM],
        out_specs=VM,
        compiler_params=pltpu.CompilerParams(vmem_limit_bytes=8 * 1024 * 1024),
        name="pair_sum",
    )(own, other)


def fold_kernel(part_ref, spot_ref, out_ref):
    shards, places, width = out_ref.shape
    capacity = places // 2
    groups = part_ref.shape[0]
    for side in range(2):
        same = [g for g in range(groups) if colour(g) == side]
        total = part_ref[same[0]].astype(F32)
        for g in same[1:]:
            total += part_ref[g].astype(F32)
        placed = lax.dot_general(
            spot_ref[side], total.astype(BF16), NN, preferred_element_type=F32
        ).astype(BF16)
        for c in range(shards):
            out_ref[c, side * capacity:(side + 1) * capacity] = placed[c * capacity:(c + 1) * capacity]


def fold(parts, spots, shards):
    places = 2 * spots.shape[1] // shards
    return pl.pallas_call(
        fold_kernel,
        out_shape=jax.ShapeDtypeStruct((shards, places, parts.shape[2]), BF16),
        in_specs=[VM, VM],
        out_specs=VM,
        compiler_params=pltpu.CompilerParams(vmem_limit_bytes=8 * 1024 * 1024),
        name="fold",
    )(parts, spots)


def collect_kernel(recv_ref, sums_ref, out_ref):
    shards, places, width = recv_ref.shape
    size = out_ref.shape[1]
    for k in range(2):
        recv = jnp.concatenate([recv_ref[2 * z + k] for z in range(shards // 2)], axis=0)
        total = lax.dot_general(sums_ref[...], recv, NN, preferred_element_type=F32).astype(BF16)
        for e in range(out_ref.shape[0]):
            out_ref[e, :, k * width:(k + 1) * width] = total[e * size:(e + 1) * size]


def collect(recv, sums, groups):
    width = recv.shape[2]
    return pl.pallas_call(
        collect_kernel,
        out_shape=jax.ShapeDtypeStruct((groups, sums.shape[0] // groups, 2 * width), BF16),
        in_specs=[VM, VM],
        out_specs=VM,
        compiler_params=pltpu.CompilerParams(vmem_limit_bytes=8 * 1024 * 1024),
        name="collect",
    )(recv, sums)


def deliver_kernel(moved_ref, ready_ref, query_ref, sem):
    copy = pltpu.make_async_copy(moved_ref, query_ref, sem)
    copy.start()
    copy.wait()


def deliver(moved, ready):
    hbm = pl.BlockSpec(memory_space=pl.ANY)
    return pl.pallas_call(
        deliver_kernel,
        out_shape=jax.ShapeDtypeStruct(moved.shape, BF16),
        in_specs=[hbm, hbm],
        out_specs=hbm,
        scratch_shapes=[pltpu.SemaphoreType.DMA],
        compiler_params=pltpu.CompilerParams(vmem_limit_bytes=8 * 1024 * 1024),
        cost_estimate=pl.CostEstimate(flops=10**9, bytes_accessed=4 * moved.size, transcendentals=0),
        name="deliver",
    )(moved, ready)


def settle_kernel(recv_ref, out_ref):
    width = recv_ref.shape[2] // 2
    for g in range(recv_ref.shape[0]):
        for k in range(2):
            at = (4 * (g // 2) + 2 * k + colour(g)) * width
            out_ref[:, at:at + width] = recv_ref[g, :, k * width:(k + 1) * width]


def settle(recv):
    groups, rows, width = recv.shape
    return pl.pallas_call(
        settle_kernel,
        out_shape=jax.ShapeDtypeStruct((rows, groups * width), BF16),
        in_specs=[VM],
        out_specs=VM,
        compiler_params=pltpu.CompilerParams(vmem_limit_bytes=8 * 1024 * 1024),
        name="settle",
    )(recv)


COLUMNS = 4


def colour(group):
    return (group // COLUMNS + group % COLUMNS) % 2


def on_device(queries, latent_cache, block_picks, out_grad):
    shards = lax.axis_size("ctx")
    groups = lax.axis_size("grp")
    block_count = latent_cache.shape[0]
    ctx = lax.axis_index("ctx")
    swap = []
    for c in range(shards):
        for e in range(groups):
            moved = c % 2 != colour(e)
            swap.append((c * groups + e, (c ^ 1) * groups + (e ^ 1) if moved else c * groups + e))
    sides = [[e for e in range(groups) if colour(e) == side] for side in range(2)]
    cores = [(c, c ^ 1) for c in range(shards)]
    moved_queries = lax.ppermute(queries, ("ctx", "grp"), swap)
    moved_grad = lax.ppermute(out_grad, ("ctx", "grp"), swap)
    spread = lax.broadcasted_iota(jnp.int32, (shards, block_picks.shape[1]), 0) == ctx
    every = lax.psum(jnp.where(spread, block_picks, 0), "ctx")
    served = serve(every, latent_cache, groups)
    fetched = lax.all_to_all(served, "ctx", split_axis=0, concat_axis=0, tiled=True)
    picked = compact(
        every, fetched, moved_queries, block_count, groups // 2
    )
    near = lax.all_to_all(
        picked, "grp", split_axis=0, concat_axis=0, tiled=True, axis_index_groups=sides
    )
    far = lax.ppermute(near, "ctx", cores)
    scores, dprobs, peaks, query_rows, grad_rows = attend_near(near, moved_queries, moved_grad)
    ds, probs, far_part = attend_scores(far, scores, dprobs, peaks, query_rows, grad_rows)
    other_part = lax.ppermute(far_part, "ctx", cores)
    near_part = attend_part(ds, probs, query_rows, grad_rows, near.shape)
    chip_part = pair_sum(near_part, other_part, groups)
    parts = lax.all_to_all(chip_part, "grp", split_axis=0, concat_axis=0, tiled=True)
    part_query_grad = attend_query(near, far, ds, chip_part)
    moved_query_grad = lax.ppermute(part_query_grad, ("ctx", "grp"), swap)
    sums, spots = plan(every, chip_part, block_count)
    placed = fold(parts, spots, shards)
    returned = lax.all_to_all(placed, "ctx", split_axis=0, concat_axis=0, tiled=True)
    owned = collect(returned, sums, groups)
    final = lax.all_to_all(owned, "grp", split_axis=0, concat_axis=0, tiled=True)
    query_grad = deliver(moved_query_grad, owned)
    return (query_grad, settle(final))


def solution(mesh):
    placed = (P("ctx", "grp"), P("ctx", None), P("ctx", None), P("ctx", "grp"))
    return jax.shard_map(
        on_device,
        mesh=mesh,
        in_specs=placed,
        out_specs=(P("ctx", "grp"), P(("ctx", "grp"), None)),
        check_vma=False,
    )
```

```python
import functools
import jax
import jax.numpy as jnp
from jax import lax
from jax.experimental import pallas as pl
from jax.experimental.pallas import tpu as pltpu
from jax.sharding import PartitionSpec as P

DL = 512
DR = 64
QBLK = 256
DK = 576
SCORE_SCALE = 192.0 ** (-0.5)
LOG2E = 1.4426950408889634
F32 = jnp.float32
BF16 = jnp.bfloat16
NT = (((1,), (1,)), ((), ()))
NN = (((1,), (0,)), ((), ()))
TN = (((0,), (0,)), ((), ()))


def near_kernel(heads, reps, near_ref, q_ref, g_ref, s_ref, dp_ref, peak_ref, qbuf, gbuf, kbuf):
    rows = near_ref.shape[0]
    for r in range(reps):
        kbuf[r * rows:(r + 1) * rows, :] = near_ref[:, r * DK:(r + 1) * DK]
    for h in range(heads):
        qbuf[h * QBLK:(h + 1) * QBLK, :] = q_ref[:, h * DK:(h + 1) * DK]
        gbuf[h * QBLK:(h + 1) * QBLK, :] = g_ref[:, h * DL:(h + 1) * DL]
    for h in range(heads):
        at = slice(h * QBLK, (h + 1) * QBLK)
        s = lax.dot_general(kbuf[...], qbuf[at, :], NT, preferred_element_type=F32)
        s_ref[:, at] = s
        dp_ref[:, at] = lax.dot_general(
            kbuf[:, :DL], gbuf[at, :], NT, preferred_element_type=F32
        )
        peak_ref[:, at] = jnp.max(s.reshape(s.shape[0] // 8, 8, QBLK), axis=0)


def scores_kernel(heads, reps, far_ref, s_ref, dp_ref, peak_ref, qbuf, gbuf, ds_ref, p_ref, far_out,
                  kbuf, sbuf, dpbuf, wbuf, pbuf):
    rows = far_ref.shape[0]
    keys = rows * reps
    for r in range(reps):
        kbuf[r * rows:(r + 1) * rows, :] = far_ref[:, r * DK:(r + 1) * DK]
    kc = 256
    nc = keys // kc
    fine = 64
    factor = SCORE_SCALE * LOG2E

    def products(h, c, peak):
        at = slice(h * QBLK, (h + 1) * QBLK)
        to = slice(c * kc, (c + 1) * kc)
        s = lax.dot_general(kbuf[to, :], qbuf[at, :], NT, preferred_element_type=F32)
        sbuf[h % 2, to, :] = s
        dpbuf[h % 2, to, :] = lax.dot_general(
            kbuf[to, :DL], gbuf[at, :], NT, preferred_element_type=F32
        )
        return jnp.maximum(peak, jnp.max(s.reshape(kc // 8, 8, QBLK), axis=0))

    def held(h, c):
        at = slice(h * QBLK, (h + 1) * QBLK)
        if c < keys // fine:
            to = slice(c * fine, (c + 1) * fine)
            return s_ref[to, at], dp_ref[to, at]
        to = slice(c * fine - keys, (c + 1) * fine - keys)
        return sbuf[h % 2, to, :], dpbuf[h % 2, to, :]

    def peak_of(h):
        return peak_ref[:, h * QBLK:(h + 1) * QBLK]

    peak = peak_of(0)
    for c in range(nc):
        peak = products(0, c, peak)
    for h in range(heads):
        at = slice(h * QBLK, (h + 1) * QBLK)
        m = jnp.max(peak, axis=0, keepdims=True)
        total = jnp.zeros((8, QBLK), F32)
        inner = jnp.zeros((8, QBLK), F32)
        for c in range(2 * keys // fine):
            to = slice(c * fine, (c + 1) * fine)
            s, dp = held(h, c)
            w = jnp.exp2((s - m) * factor)
            wbuf[to, :] = w
            total += jnp.sum(w.reshape(fine // 8, 8, QBLK), axis=0)
            inner += jnp.sum((w * dp).reshape(fine // 8, 8, QBLK), axis=0)
        inv = 1.0 / jnp.sum(total, axis=0, keepdims=True)
        inner = jnp.sum(inner, axis=0, keepdims=True) * inv
        if h + 1 < heads:
            peak = peak_of(h + 1)
        for c in range(2 * keys // fine):
            to = slice(c * fine, (c + 1) * fine)
            a = wbuf[to, :] * inv
            d = a * ((held(h, c)[1] - inner) * SCORE_SCALE)
            if c < keys // fine:
                p_ref[to, at] = a.astype(BF16)
            else:
                pbuf[c * fine - keys:(c + 1) * fine - keys, at] = a.astype(BF16)
            ds_ref[to, at] = d.astype(BF16)
            if h + 1 < heads and (c + 1) % (2 * keys // fine // nc) == 0:
                peak = products(h + 1, (c + 1) // (2 * keys // fine // nc) - 1, peak)
    part(heads, reps, rows, ds_ref, keys, pbuf, qbuf, gbuf, far_out)


def part(heads, reps, rows, ds_ref, base, p_ref, qbuf, gbuf, out_ref):
    for r in range(reps):
        ds = ds_ref[base + r * rows:base + (r + 1) * rows, :]
        p = p_ref[r * rows:(r + 1) * rows, :]
        kp = lax.dot_general(ds, qbuf[...], NN, preferred_element_type=F32)
        vp = lax.dot_general(p, gbuf[...], NN, preferred_element_type=F32)
        out_ref[:, r * DK:r * DK + DL] = (kp[:, :DL] + vp).astype(BF16)
        out_ref[:, r * DK + DL:(r + 1) * DK] = kp[:, DL:].astype(BF16)


def part_kernel(heads, reps, ds_ref, p_ref, qbuf, gbuf, near_out):
    part(heads, reps, near_out.shape[0], ds_ref, 0, p_ref, qbuf, gbuf, near_out)


def query_kernel(heads, reps, near_ref, far_ref, ds_ref, ready_ref, dq_ref, ktbuf):
    rows = near_ref.shape[0]
    for half, ref in enumerate((near_ref, far_ref)):
        for r in range(reps):
            at = (half * reps + r) * rows
            ktbuf[:, at:at + rows] = ref[:, r * DK:(r + 1) * DK].T
    for h in range(heads):
        dqt = lax.dot_general(ktbuf[...], ds_ref[:, h * QBLK:(h + 1) * QBLK], NN, preferred_element_type=F32)
        dq_ref[:, h * DK:(h + 1) * DK] = dqt.T.astype(BF16)


VM = pl.BlockSpec(memory_space=pltpu.VMEM)


def attend_near(near, q, g):
    rows = near.shape[0]
    reps = near.shape[1] // DK
    heads = q.shape[1] // DK
    keys = rows * reps
    wide = heads * QBLK
    return pl.pallas_call(
        functools.partial(near_kernel, heads, reps),
        out_shape=(
            jax.ShapeDtypeStruct((keys, wide), F32),
            jax.ShapeDtypeStruct((keys, wide), F32),
            jax.ShapeDtypeStruct((8, wide), F32),
            jax.ShapeDtypeStruct((wide, DK), BF16),
            jax.ShapeDtypeStruct((wide, DL), BF16),
        ),
        in_specs=[VM] * 3,
        out_specs=(VM,) * 5,
        scratch_shapes=[pltpu.VMEM((keys, DK), BF16)],
        compiler_params=pltpu.CompilerParams(vmem_limit_bytes=20 * 1024 * 1024),
        cost_estimate=pl.CostEstimate(
            flops=4 * keys * wide * DK, bytes_accessed=16 * near.size, transcendentals=0
        ),
        name="attend_near",
    )(near, q, g)


def attend_scores(far, scores, dprobs, peaks, qs, gs):
    rows = far.shape[0]
    reps = far.shape[1] // DK
    heads = qs.shape[0] // QBLK
    keys = rows * reps
    wide = heads * QBLK
    return pl.pallas_call(
        functools.partial(scores_kernel, heads, reps),
        out_shape=(
            jax.ShapeDtypeStruct((2 * keys, wide), BF16),
            jax.ShapeDtypeStruct((keys, wide), BF16),
            jax.ShapeDtypeStruct(far.shape, BF16),
        ),
        in_specs=[VM] * 6,
        out_specs=(VM,) * 3,
        scratch_shapes=[
            pltpu.VMEM((keys, DK), BF16),
            pltpu.VMEM((2, keys, QBLK), F32),
            pltpu.VMEM((2, keys, QBLK), F32),
            pltpu.VMEM((2 * keys, QBLK), F32),
            pltpu.VMEM((keys, wide), BF16),
        ],
        compiler_params=pltpu.CompilerParams(vmem_limit_bytes=34 * 1024 * 1024),
        cost_estimate=pl.CostEstimate(
            flops=6 * keys * wide * DK, bytes_accessed=16 * far.size, transcendentals=keys * wide
        ),
        name="attend_scores",
    )(far, scores, dprobs, peaks, qs, gs)


def attend_part(ds, p, qs, gs, shape):
    heads = ds.shape[1] // QBLK
    return pl.pallas_call(
        functools.partial(part_kernel, heads, shape[1] // DK),
        out_shape=jax.ShapeDtypeStruct(shape, BF16),
        in_specs=[VM] * 4,
        out_specs=VM,
        compiler_params=pltpu.CompilerParams(vmem_limit_bytes=16 * 1024 * 1024),
        cost_estimate=pl.CostEstimate(flops=4 * ds.shape[0] // 2 * ds.shape[1] * DK, bytes_accessed=4 * ds.size, transcendentals=0),
        name="attend_part",
    )(ds, p, qs, gs)


def attend_query(near, far, ds, ready):
    heads = ds.shape[1] // QBLK
    reps = near.shape[1] // DK
    return pl.pallas_call(
        functools.partial(query_kernel, heads, reps),
        out_shape=jax.ShapeDtypeStruct((QBLK, heads * DK), BF16),
        in_specs=[VM] * 3 + [pl.BlockSpec(memory_space=pl.ANY)],
        out_specs=VM,
        scratch_shapes=[pltpu.VMEM((DK, ds.shape[0]), BF16)],
        compiler_params=pltpu.CompilerParams(vmem_limit_bytes=14 * 1024 * 1024),
        cost_estimate=pl.CostEstimate(flops=2 * ds.size * DK, bytes_accessed=4 * ds.size, transcendentals=0),
        name="attend_query",
    )(near, far, ds, ready)


def shifted(values, size):
    return lax.shift_right_logical(values, size.bit_length() - 1)


def serve_kernel(picks_ref, cache_ref, out_ref, rows_ref, slice_ref, held_ref, sems):
    shards, capacity, width = held_ref.shape
    blocks = cache_ref.shape[0]
    me = lax.axis_index("ctx")
    group = lax.axis_index("grp")
    pull = pltpu.make_async_copy(picks_ref, rows_ref, sems.at[0])
    pull.start()
    start = pl.multiple_of((group // 2) * (2 * width), 128)
    fetch = pltpu.make_async_copy(cache_ref.at[:, pl.ds(start, 2 * width)], slice_ref, sems.at[1])
    fetch.start()
    asking = shards // 2
    slots = asking * capacity
    per = picks_ref.shape[1]
    total = asking * per
    mark = colour(group)
    first = lax.broadcasted_iota(jnp.int32, (per, per), 0)
    second = lax.broadcasted_iota(jnp.int32, (per, per), 1)
    before = (first < second).astype(BF16)
    slot = lax.broadcasted_iota(jnp.int32, (slots, total), 0)
    asker = shifted(lax.broadcasted_iota(jnp.int32, (slots, total), 1), per)
    block = lax.broadcasted_iota(jnp.int32, (blocks, total), 0)
    pull.wait()
    rows = [rows_ref[pl.ds(2 * z + mark, 1), :] for z in range(asking)]
    picks = jnp.concatenate(rows, axis=0)
    mine = shifted(picks, blocks) == me
    rank = lax.dot_general(mine.astype(BF16), before, NN, preferred_element_type=F32)
    spots = jnp.where(mine, rank.astype(jnp.int32), capacity)
    spot = jnp.concatenate([spots[z:z + 1] for z in range(asking)], axis=1)
    within = jnp.concatenate([rows[z] & (blocks - 1) for z in range(asking)], axis=1)
    left = (slot == asker * capacity + spot) & (spot < capacity)
    right = (block == within).astype(BF16)
    chosen = lax.dot_general(left.astype(BF16), right, NT, preferred_element_type=F32).astype(BF16)
    fetch.wait()
    copies = []
    for half in range(2):
        span = slice(half * slots // 2, (half + 1) * slots // 2)
        served = lax.dot_general(
            chosen[span], slice_ref[...], NN, preferred_element_type=F32
        ).astype(BF16)
        for z in range(asking // 2):
            part = served[z * capacity:(z + 1) * capacity]
            at = half * asking + 2 * z
            held_ref[at] = part[:, :width]
            held_ref[at + 1] = part[:, width:]
        span = pl.ds(half * asking, asking)
        copies.append(pltpu.make_async_copy(held_ref.at[span], out_ref.at[span], sems.at[2 + half]))
        copies[-1].start()
    for copy in copies:
        copy.wait()


def serve(picks, cache, groups):
    blocks, whole = cache.shape
    shards, per = picks.shape
    width = whole // groups
    capacity = 2 * per // shards
    shape = (shards, capacity, width)
    return pl.pallas_call(
        serve_kernel,
        out_shape=jax.ShapeDtypeStruct(shape, BF16),
        in_specs=[pl.BlockSpec(memory_space=pl.ANY)] * 2,
        out_specs=pl.BlockSpec(memory_space=pl.ANY),
        scratch_shapes=[
            pltpu.VMEM((shards, per), jnp.int32),
            pltpu.VMEM((blocks, 2 * width), BF16),
            pltpu.VMEM(shape, BF16),
            pltpu.SemaphoreType.DMA((4,)),
        ],
        compiler_params=pltpu.CompilerParams(vmem_limit_bytes=58 * 1024 * 1024),
        name="serve",
    )(picks, cache)


def spots_of(picks, shards, capacity, block_count):
    slots = shards * capacity
    per = picks.shape[1]
    holder = shifted(picks, block_count)
    first = lax.broadcasted_iota(jnp.int32, (per, per), 0)
    second = lax.broadcasted_iota(jnp.int32, (per, per), 1)
    shard = lax.broadcasted_iota(jnp.int32, (shards, per), 0)
    held = shard == holder
    before = (first < second).astype(BF16)
    counts = lax.dot_general(held.astype(BF16), before, NN, preferred_element_type=F32)
    rank = jnp.sum(jnp.where(held, counts, 0.0), axis=0, keepdims=True).astype(jnp.int32)
    slot = lax.broadcasted_iota(jnp.int32, (slots, per), 0)
    return (slot == holder * capacity + rank).astype(BF16)


def compact_kernel(block_count, copies, picks_ref, recv_ref, first_ready, second_ready, out_ref):
    shards, capacity, width = recv_ref.shape
    per = picks_ref.shape[1]
    row = lax.axis_index("ctx") // 2 * 2 + colour(lax.axis_index("grp"))
    spots = spots_of(picks_ref[pl.ds(row, 1), :], shards, capacity, block_count)
    recv = jnp.concatenate([recv_ref[c] for c in range(shards)], axis=0)
    picked = lax.dot_general(spots, recv, TN, preferred_element_type=F32).astype(BF16)
    for e in range(copies):
        out_ref[e * per:(e + 1) * per, :] = picked


def compact(picks, recv, ready, block_count, copies):
    per = picks.shape[1]
    hold = pl.BlockSpec(memory_space=pl.ANY)
    return pl.pallas_call(
        functools.partial(compact_kernel, block_count, copies),
        out_shape=jax.ShapeDtypeStruct((copies * per, recv.shape[2]), BF16),
        in_specs=[VM, VM, hold, hold],
        out_specs=VM,
        compiler_params=pltpu.CompilerParams(vmem_limit_bytes=8 * 1024 * 1024),
        name="compact",
    )(picks, recv, *ready)


def plan_kernel(block_count, picks_ref, ready_ref, sums_ref, spots_ref):
    shards, per = picks_ref.shape
    total = shards * per
    slots = sums_ref.shape[1]
    capacity = slots // shards
    me = lax.axis_index("ctx")
    picks = jnp.concatenate([picks_ref[c:c + 1, :] for c in range(shards)], axis=1)
    mine = (picks // block_count) == me
    within = picks % block_count
    first = lax.broadcasted_iota(jnp.int32, (total, total), 0)
    second = lax.broadcasted_iota(jnp.int32, (total, total), 1)
    before = ((first // per == second // per) & (first < second)).astype(BF16)
    marks = jnp.broadcast_to(mine.astype(F32), (8, total)).astype(BF16)
    rank = lax.dot_general(marks, before, NN, preferred_element_type=F32)[:1].astype(jnp.int32)
    slot = lax.broadcasted_iota(jnp.int32, (slots, total), 0)
    asker = lax.broadcasted_iota(jnp.int32, (slots, total), 1) // per
    spot = jnp.where(mine, rank, capacity)
    left = ((slot // capacity == asker) & (slot % capacity == spot)).astype(BF16)
    block = lax.broadcasted_iota(jnp.int32, (block_count, total), 0)
    right = (block == within).astype(BF16)
    sums_ref[...] = lax.dot_general(right, left, NT, preferred_element_type=F32).astype(BF16)
    for side in range(2):
        row = me // 2 * 2 + side
        spots_ref[side] = spots_of(picks_ref[pl.ds(row, 1), :], shards, capacity, block_count)


def plan(picks, ready, block_count):
    shards, per = picks.shape
    slots = 2 * per
    return pl.pallas_call(
        functools.partial(plan_kernel, block_count),
        out_shape=(
            jax.ShapeDtypeStruct((block_count, slots), BF16),
            jax.ShapeDtypeStruct((2, slots, per), BF16),
        ),
        in_specs=[VM, pl.BlockSpec(memory_space=pl.ANY)],
        out_specs=(VM, VM),
        compiler_params=pltpu.CompilerParams(vmem_limit_bytes=8 * 1024 * 1024),
        cost_estimate=pl.CostEstimate(flops=10**9, bytes_accessed=10**6, transcendentals=0),
        name="plan",
    )(picks, ready)


def pair_kernel(own_ref, other_ref, out_ref, held_ref, sems):
    groups, per, width = held_ref.shape
    parts = sems.shape[0]
    size = groups // parts
    copies = []
    for part in range(parts):
        for g in range(part * size, (part + 1) * size):
            rows = slice(g // 2 * per, (g // 2 + 1) * per)
            at = slice(colour(g) * width, (colour(g) + 1) * width)
            both = own_ref[rows, at].astype(F32) + other_ref[rows, at].astype(F32)
            held_ref[g] = both.astype(BF16)
        span = pl.ds(part * size, size)
        copies.append(pltpu.make_async_copy(held_ref.at[span], out_ref.at[span], sems.at[part]))
        copies[-1].start()
    for copy in copies:
        copy.wait()


def pair_sum(own, other, groups):
    rows, width = own.shape
    shape = (groups, 2 * rows // groups, width // 2)
    return pl.pallas_call(
        pair_kernel,
        out_shape=jax.ShapeDtypeStruct(shape, BF16),
        in_specs=[VM, VM],
        out_specs=pl.BlockSpec(memory_space=pl.ANY),
        scratch_shapes=[pltpu.VMEM(shape, BF16), pltpu.SemaphoreType.DMA((4,))],
        compiler_params=pltpu.CompilerParams(vmem_limit_bytes=8 * 1024 * 1024),
        name="pair_sum",
    )(own, other)


def fold_kernel(part_ref, spot_ref, out_ref):
    shards, places, width = out_ref.shape
    capacity = places // 2
    groups = part_ref.shape[0]
    for side in range(2):
        same = [g for g in range(groups) if colour(g) == side]
        total = part_ref[same[0]].astype(F32)
        for g in same[1:]:
            total += part_ref[g].astype(F32)
        placed = lax.dot_general(
            spot_ref[side], total.astype(BF16), NN, preferred_element_type=F32
        ).astype(BF16)
        for c in range(shards):
            out_ref[c, side * capacity:(side + 1) * capacity] = placed[c * capacity:(c + 1) * capacity]


def fold(parts, spots, shards):
    places = 2 * spots.shape[1] // shards
    return pl.pallas_call(
        fold_kernel,
        out_shape=jax.ShapeDtypeStruct((shards, places, parts.shape[2]), BF16),
        in_specs=[VM, VM],
        out_specs=VM,
        compiler_params=pltpu.CompilerParams(vmem_limit_bytes=8 * 1024 * 1024),
        name="fold",
    )(parts, spots)


def collect_kernel(recv_ref, sums_ref, out_ref):
    shards, places, width = recv_ref.shape
    size = out_ref.shape[1]
    for k in range(2):
        recv = jnp.concatenate([recv_ref[2 * z + k] for z in range(shards // 2)], axis=0)
        total = lax.dot_general(sums_ref[...], recv, NN, preferred_element_type=F32).astype(BF16)
        for e in range(out_ref.shape[0]):
            out_ref[e, :, k * width:(k + 1) * width] = total[e * size:(e + 1) * size]


def collect(recv, sums, groups):
    width = recv.shape[2]
    return pl.pallas_call(
        collect_kernel,
        out_shape=jax.ShapeDtypeStruct((groups, sums.shape[0] // groups, 2 * width), BF16),
        in_specs=[VM, VM],
        out_specs=VM,
        compiler_params=pltpu.CompilerParams(vmem_limit_bytes=8 * 1024 * 1024),
        name="collect",
    )(recv, sums)


def deliver_kernel(moved_ref, ready_ref, query_ref, sem):
    copy = pltpu.make_async_copy(moved_ref, query_ref, sem)
    copy.start()
    copy.wait()


def deliver(moved, ready):
    hbm = pl.BlockSpec(memory_space=pl.ANY)
    return pl.pallas_call(
        deliver_kernel,
        out_shape=jax.ShapeDtypeStruct(moved.shape, BF16),
        in_specs=[hbm, hbm],
        out_specs=hbm,
        scratch_shapes=[pltpu.SemaphoreType.DMA],
        compiler_params=pltpu.CompilerParams(vmem_limit_bytes=8 * 1024 * 1024),
        cost_estimate=pl.CostEstimate(flops=10**9, bytes_accessed=4 * moved.size, transcendentals=0),
        name="deliver",
    )(moved, ready)


def settle_kernel(recv_ref, out_ref):
    width = recv_ref.shape[2] // 2
    for g in range(recv_ref.shape[0]):
        for k in range(2):
            at = (4 * (g // 2) + 2 * k + colour(g)) * width
            out_ref[:, at:at + width] = recv_ref[g, :, k * width:(k + 1) * width]


def settle(recv):
    groups, rows, width = recv.shape
    return pl.pallas_call(
        settle_kernel,
        out_shape=jax.ShapeDtypeStruct((rows, groups * width), BF16),
        in_specs=[VM],
        out_specs=VM,
        compiler_params=pltpu.CompilerParams(vmem_limit_bytes=8 * 1024 * 1024),
        name="settle",
    )(recv)


COLUMNS = 4


def colour(group):
    return (group % COLUMNS + 1) // 2 % 2


def on_device(queries, latent_cache, block_picks, out_grad):
    shards = lax.axis_size("ctx")
    groups = lax.axis_size("grp")
    block_count = latent_cache.shape[0]
    ctx = lax.axis_index("ctx")
    swap = []
    for c in range(shards):
        for e in range(groups):
            moved = c % 2 != colour(e)
            swap.append((c * groups + e, (c ^ 1) * groups + (e ^ 1) if moved else c * groups + e))
    sides = [[e for e in range(groups) if colour(e) == side] for side in range(2)]
    cores = [(c, c ^ 1) for c in range(shards)]
    moved_queries = lax.ppermute(queries, ("ctx", "grp"), swap)
    moved_grad = lax.ppermute(out_grad, ("ctx", "grp"), swap)
    spread = lax.broadcasted_iota(jnp.int32, (shards, block_picks.shape[1]), 0) == ctx
    every = lax.psum(jnp.where(spread, block_picks, 0), "ctx")
    served = serve(every, latent_cache, groups)
    fetched = lax.all_to_all(served, "ctx", split_axis=0, concat_axis=0, tiled=True)
    picked = compact(
        every, fetched, (moved_queries, moved_grad), block_count, groups // 2
    )
    near = lax.all_to_all(
        picked, "grp", split_axis=0, concat_axis=0, tiled=True, axis_index_groups=sides
    )
    far = lax.ppermute(near, "ctx", cores)
    scores, dprobs, peaks, query_rows, grad_rows = attend_near(near, moved_queries, moved_grad)
    ds, probs, far_part = attend_scores(far, scores, dprobs, peaks, query_rows, grad_rows)
    other_part = lax.ppermute(far_part, "ctx", cores)
    near_part = attend_part(ds, probs, query_rows, grad_rows, near.shape)
    chip_part = pair_sum(near_part, other_part, groups)
    parts = lax.all_to_all(chip_part, "grp", split_axis=0, concat_axis=0, tiled=True)
    part_query_grad = attend_query(near, far, ds, chip_part)
    moved_query_grad = lax.ppermute(part_query_grad, ("ctx", "grp"), swap)
    sums, spots = plan(every, chip_part, block_count)
    placed = fold(parts, spots, shards)
    returned = lax.all_to_all(placed, "ctx", split_axis=0, concat_axis=0, tiled=True)
    owned = collect(returned, sums, groups)
    final = lax.all_to_all(owned, "grp", split_axis=0, concat_axis=0, tiled=True)
    query_grad = deliver(moved_query_grad, owned)
    return (query_grad, settle(final))


def solution(mesh):
    placed = (P("ctx", "grp"), P("ctx", None), P("ctx", None), P("ctx", "grp"))
    return jax.shard_map(
        on_device,
        mesh=mesh,
        in_specs=placed,
        out_specs=(P("ctx", "grp"), P(("ctx", "grp"), None)),
        check_vma=False,
    )
```
